256 devices in a mesh: gx: 32 (over y_hi, z, core), gy: 8 (over y_lo, x).
Axes of the slice: x: 4, y: 4 (y_hi: 2, y_lo: 2; y = y_hi * 2 + y_lo), z: 8, core: 2. Of those that a mesh axis runs over, the one named last changes fastest.
Arguments:
- target: float32 [512, 128, 1024], P('gx', None, 'gy'), may hold values from -6 to 6
- plane_xy: float32 [32, 512, 1024], P(None, 'gx', 'gy'), may hold values from 0.4 to 1.6
- plane_xz: float32 [32, 512, 128], P(None, 'gx', 'gy'), may hold values from 0.4 to 1.6
- plane_yz: float32 [32, 128, 1024], P(None, 'gx', 'gy'), may hold values from 0.4 to 1.6
- first_xy: float32 [32, 512, 1024], P(None, 'gx', 'gy'), may hold values from -6 to 6
- first_xz: float32 [32, 512, 128], P(None, 'gx', 'gy'), may hold values from -6 to 6
- first_yz: float32 [32, 128, 1024], P(None, 'gx', 'gy'), may hold values from -6 to 6
- second_xy: float32 [32, 512, 1024], P(None, 'gx', 'gy'), may hold values from 0.5 to 8
- second_xz: float32 [32, 512, 128], P(None, 'gx', 'gy'), may hold values from 0.5 to 8
- second_yz: float32 [32, 128, 1024], P(None, 'gx', 'gy'), may hold values from 0.5 to 8
- w_hidden: bfloat16 [32, 32], replicated, may hold values from -1 to 1
- b_hidden: float32 [32], replicated, may hold values from -3 to 3
- w_output: bfloat16 [32], replicated, may hold values from -1 to 1
- b_output: float32 [1], replicated, may hold values from -3 to 3
Outputs:
- updated_xy: float32 [32, 512, 1024], P(None, 'gx', 'gy')
- updated_xz: float32 [32, 512, 128], P(None, 'gx', 'gy')
- updated_yz: float32 [32, 128, 1024], P(None, 'gx', 'gy')
- mean_xy: float32 [32, 512, 1024], P(None, 'gx', 'gy')
- mean_xz: float32 [32, 512, 128], P(None, 'gx', 'gy')
- mean_yz: float32 [32, 128, 1024], P(None, 'gx', 'gy')
- square_xy: float32 [32, 512, 1024], P(None, 'gx', 'gy')
- square_xz: float32 [32, 512, 128], P(None, 'gx', 'gy')
- square_yz: float32 [32, 128, 1024], P(None, 'gx', 'gy')
The draws below stay inside these ranges and needn't reach their ends.
All inputs are finite; a program needn't handle non-finite values.
Results may differ from the reference program's by a relative error of at most 0.00053.
Values sent between devices are 32-bit elements; how exact they have to be, the bound alone decides.
A program may use at most 64 MiB of HBM per device.

```python
import math
import jax
import jax.numpy as jnp
from jax import lax

C = 32
HIDDEN_SIZE = 32
Z = 128
STEPS = 2
START = 20
X = 512
Y = 1024


def shard_levels(key, extent, shards, least, top_value):
    gain = 1.0
    for dim, parts in shards:
        steps = jax.random.uniform(jax.random.fold_in(jax.random.fold_in(key, 6), dim), (parts,), jnp.float32, least / len(shards), top_value / len(shards))
        gain = gain * jnp.repeat(jnp.exp(steps), extent[dim] // parts).reshape((-1,) + (1,) * (len(extent) - 1 - dim))
    return gain


def centred(key, dims, width, limit, pieces=(), kind=jnp.bfloat16):
    array = width * jax.random.normal(key, dims, jnp.float32)
    if pieces:
        array = array * shard_levels(key, dims, pieces, -0.22, 0.18)
    return jnp.clip(array, -limit, limit).astype(kind)


def setup_inputs(seed: int = 0) -> dict:
    key_of = jax.random.split(jax.random.key(seed), 15)
    return {
        "target": centred(key_of[0], (X, Z, Y), 1.0, 6.0, ((0, 32), (2, 8)), jnp.float32),
        "plane_xy": jnp.clip(0.4 + 1.2 * jax.random.uniform(key_of[1], (C, X, Y), jnp.float32) ** shard_levels(key_of[1], (C, X, Y), ((1, 32), (2, 8)), -0.2, 0.2), 0.4, 1.6),
        "plane_xz": jnp.clip(0.4 + 1.2 * jax.random.uniform(key_of[2], (C, X, Z), jnp.float32) ** shard_levels(key_of[2], (C, X, Z), ((1, 32), (2, 8)), -0.2, 0.2), 0.4, 1.6),
        "plane_yz": jnp.clip(0.4 + 1.2 * jax.random.uniform(key_of[3], (C, Z, Y), jnp.float32) ** shard_levels(key_of[3], (C, Z, Y), ((1, 32), (2, 8)), -0.2, 0.2), 0.4, 1.6),
        "first_xy": centred(key_of[4], (C, X, Y), 1.0, 6.0, ((1, 32), (2, 8)), jnp.float32),
        "first_xz": centred(key_of[5], (C, X, Z), 1.0, 6.0, ((1, 32), (2, 8)), jnp.float32),
        "first_yz": centred(key_of[6], (C, Z, Y), 1.0, 6.0, ((1, 32), (2, 8)), jnp.float32),
        "second_xy": jnp.clip(jnp.exp(math.log(8.0) - 2.7725887 * jax.random.uniform(key_of[7], (C, X, Y), jnp.float32) ** shard_levels(key_of[7], (C, X, Y), ((1, 32), (2, 8)), -0.2, 0.2)), 0.5, 8.0),
        "second_xz": jnp.clip(jnp.exp(math.log(8.0) - 2.7725887 * jax.random.uniform(key_of[8], (C, X, Z), jnp.float32) ** shard_levels(key_of[8], (C, X, Z), ((1, 32), (2, 8)), -0.2, 0.2)), 0.5, 8.0),
        "second_yz": jnp.clip(jnp.exp(math.log(8.0) - 2.7725887 * jax.random.uniform(key_of[9], (C, Z, Y), jnp.float32) ** shard_levels(key_of[9], (C, Z, Y), ((1, 32), (2, 8)), -0.2, 0.2)), 0.5, 8.0),
        "w_hidden": centred(key_of[10], (C, HIDDEN_SIZE), C ** -0.5, 1.0),
        "b_hidden": centred(key_of[11], (HIDDEN_SIZE,), 0.5, 3.0, (), jnp.float32),
        "w_output": centred(key_of[12], (HIDDEN_SIZE,), HIDDEN_SIZE ** -0.5, 1.0),
        "b_output": centred(key_of[13], (1,), 0.5, 3.0, (), jnp.float32),
    }


SMOOTHING = 0.5
BETA_ONE = 0.9
BETA_TWO = 0.99
LEARN_RATE = 0.01
EPSILON = 1e-08

def rounded(values):
    return lax.optimization_barrier(values.astype(jnp.bfloat16)).astype(jnp.float32)

def smooth(plane):
    down = plane[:, 1:, :] - plane[:, :-1, :]
    down = jnp.pad(down, ((0, 0), (1, 1), (0, 0)))
    across = plane[:, :, 1:] - plane[:, :, :-1]
    across = jnp.pad(across, ((0, 0), (0, 0), (1, 1)))
    return 2.0 * SMOOTHING * (down[:, :-1, :] - down[:, 1:, :] + across[:, :, :-1] - across[:, :, 1:])

def data_grads(target, plane_xy, plane_xz, plane_yz, w_hidden, b_hidden, w_output, b_output):
    weights_in = w_hidden.astype(jnp.float32)
    weights_out = w_output.astype(jnp.float32)

    def one_row(running, inputs):
        target_row, row_xy, row_xz = inputs
        cross = row_xz[:, :, None] * plane_yz
        features = rounded(row_xy[:, None, :] * cross)
        preact = jnp.einsum('ch,czy->hzy', weights_in, features) + b_hidden[:, None, None]
        sigma = jax.nn.sigmoid(preact)
        hidden = rounded(preact * sigma)
        output = jnp.einsum('h,hzy->zy', weights_out, hidden) + b_output[0]
        residual = output - target_row
        back_hidden = rounded(weights_out[:, None, None] * residual[None] * (sigma * (1.0 + preact * (1.0 - sigma))))
        back_feature = jnp.einsum('ch,hzy->czy', weights_in, back_hidden)
        grad_row_xy = lax.optimization_barrier(jnp.sum(back_feature * cross, axis=1))
        with_xy = back_feature * row_xy[:, None, :]
        grad_row_xz = lax.optimization_barrier(jnp.sum(with_xy * plane_yz, axis=2))
        running = running + with_xy * row_xz[:, :, None]
        return (running, (grad_row_xy, grad_row_xz))
    start = jnp.zeros(plane_yz.shape, jnp.float32)
    grad_yz, (rows_xy, rows_xz) = lax.scan(one_row, start, (target, jnp.moveaxis(plane_xy, 1, 0), jnp.moveaxis(plane_xz, 1, 0)))
    return (jnp.moveaxis(rows_xy, 0, 1), jnp.moveaxis(rows_xz, 0, 1), grad_yz)

def adam(plane, first, second, grads, count):
    first = BETA_ONE * first + (1.0 - BETA_ONE) * grads
    second = BETA_TWO * second + (1.0 - BETA_TWO) * grads * grads
    corr_one = 1.0 - BETA_ONE ** count
    corr_two = 1.0 - BETA_TWO ** count
    plane = plane - LEARN_RATE * (first / corr_one) / (jnp.sqrt(second / corr_two) + EPSILON)
    return (plane, first, second)

def reference(target, plane_xy, plane_xz, plane_yz, first_xy, first_xz, first_yz, second_xy, second_xz, second_yz, w_hidden, b_hidden, w_output, b_output):
    for iteration in range(STEPS):
        grad_xy, grad_xz, grad_yz = data_grads(target, plane_xy, plane_xz, plane_yz, w_hidden, b_hidden, w_output, b_output)
        grad_xy = grad_xy + smooth(plane_xy)
        grad_xz = grad_xz + smooth(plane_xz)
        grad_yz = grad_yz + smooth(plane_yz)
        count = START + iteration + 1
        plane_xy, first_xy, second_xy = adam(plane_xy, first_xy, second_xy, grad_xy, count)
        plane_xz, first_xz, second_xz = adam(plane_xz, first_xz, second_xz, grad_xz, count)
        plane_yz, first_yz, second_yz = adam(plane_yz, first_yz, second_yz, grad_yz, count)
    return (plane_xy, plane_xz, plane_yz, first_xy, first_xz, first_yz, second_xy, second_xz, second_yz)
```

```python
import jax
import jax.numpy as jnp
from jax import lax
from jax.experimental import pallas as pl
from jax.experimental.pallas import tpu as pltpu
from jax.sharding import PartitionSpec as P

STEPS = 2
START = 20


SMOOTHING = 0.5
BETA_ONE = 0.9
BETA_TWO = 0.99
LEARN_RATE = 0.01
EPSILON = 1e-08
NX = 16
NB = 16
F32 = jnp.float32
BF = jnp.bfloat16


def padded_2(x, sides, width):
    for axis, dim in sides:
        peers, length = (lax.axis_size(axis), x.shape[dim])
        up = [(i, (i + 1) % peers) for i in range(peers - 1)]
        down = [(j, i) for i, j in up]
        last = lax.slice_in_dim(x, length - width, length, axis=dim)
        first = lax.slice_in_dim(x, 0, width, axis=dim)
        before = lax.ppermute(last, axis, up)
        after = lax.ppermute(first, axis, down)
        x = jnp.concatenate([before, x, after], axis=dim)
    return x


def smooth(plane):
    padded = padded_2(plane, (("gx", 1), ("gy", 2)), 1)
    down = padded[:, 1:, 1:-1] - padded[:, :-1, 1:-1]
    across = padded[:, 1:-1, 1:] - padded[:, 1:-1, :-1]
    row_count = down.shape[1]
    col_count = across.shape[2]
    row_places = jnp.arange(row_count)
    col_places = jnp.arange(col_count)
    lowest_x = lax.axis_index("gx") == 0
    highest_x = lax.axis_index("gx") == lax.axis_size("gx") - 1
    lowest_y = lax.axis_index("gy") == 0
    highest_y = lax.axis_index("gy") == lax.axis_size("gy") - 1
    row_keeps = jnp.where(
        (row_places == 0) & lowest_x | (row_places == row_count - 1) & highest_x, 0.0, 1.0
    )
    col_keeps = jnp.where(
        (col_places == 0) & lowest_y | (col_places == col_count - 1) & highest_y, 0.0, 1.0
    )
    down = down * row_keeps[None, :, None]
    across = across * col_keeps[None, None, :]
    return (
        2.0 * SMOOTHING * (down[:, :-1, :] - down[:, 1:, :] + across[:, :, :-1] - across[:, :, 1:])
    )


def grad_block(zb, tgt, xy, xz, yz, w1, w2, wo, bh, wv, b0, accxy, gxz, gyz, fbuf, dbuf, rbuf):
    wide = NX * 128
    xt = jnp.transpose(xz[zb])
    h1 = xt.astype(BF)
    r1 = xt - h1.astype(F32)
    h2 = r1.astype(BF)
    h3 = (r1 - h2.astype(F32)).astype(BF)
    parts = jnp.concatenate([h1, h2, h3], axis=1)
    place = lax.broadcasted_iota(jnp.int32, (3 * NX, 128), 0) % NX
    yzt = yz[pl.ds(zb * 8, 8)].reshape(256, 128)
    for x in range(NX):
        col = jnp.dot(parts, (place == x).astype(BF), preferred_element_type=F32)
        f = ((col * yzt).reshape(8, 32, 128) * xy[x][None]).reshape(256, 128)
        fbuf[:, x * 128 : (x + 1) * 128] = f
    pre = jnp.dot(w1[...], fbuf[...].astype(BF), preferred_element_type=F32)
    q = pre.reshape(8, 32, wide) + jnp.concatenate([bh[...]] * NX, axis=-1)[None]
    u = 1.0 + jnp.tanh(q)
    h = q * u
    dbuf[...] = (u + h * (2.0 - u)) * jnp.concatenate([wv[...]] * NX, axis=-1)[None]
    out = jnp.dot(wo[...], h.reshape(256, wide).astype(BF), preferred_element_type=F32)[:8]
    for x in range(NX):
        rbuf[:, x * 128 : (x + 1) * 128] = (
            out[:, x * 128 : (x + 1) * 128] + b0 - tgt[x, pl.ds(zb * 8, 8), :]
        )
    d = (dbuf[...] * rbuf[...][:, None, :]).reshape(256, wide)
    s = jnp.dot(w2[...], d.astype(BF), preferred_element_type=F32) * fbuf[...]
    acc = None
    for x in range(NX):
        sx = s[:, x * 128 : (x + 1) * 128]
        acc = sx if acc is None else acc + sx
        accxy[x] += jnp.sum(sx.reshape(8, 32, 128), axis=0)
        gxz[zb, x : x + 1, :] = jnp.sum(sx, axis=-1).reshape(1, 256)
    gyz[pl.ds(zb * 8, 8)] = acc.reshape(8, 32, 128)


def grad_kernel(tgt, xy, xz, yz, w1, w2, wo, bh, wv, bo, gxy, gxz, gyz, fbuf, dbuf, rbuf):
    gxy[...] = jnp.zeros_like(gxy)
    b0 = bo[0]

    def step(zb, carry):
        grad_block(zb, tgt, xy, xz, yz, w1, w2, wo, bh, wv, b0, gxy, gxz, gyz, fbuf, dbuf, rbuf)
        return carry

    lax.fori_loop(0, NB, step, 0)


def weights(w_hidden, b_hidden, w_output):
    eye = jnp.eye(8, dtype=F32)
    wf = w_hidden.astype(F32)
    w1 = jnp.kron(eye, 0.5 * wf.T).astype(BF)
    w2 = jnp.kron(eye, wf).astype(BF)
    wof = w_output.astype(F32)
    wo = jnp.pad(jnp.kron(eye, wof[None, :]), ((0, 8), (0, 0))).astype(BF)
    bh = jnp.broadcast_to((0.5 * b_hidden)[:, None], (32, 128))
    wv = jnp.broadcast_to((0.5 * wof)[:, None], (32, 128))
    return w1, w2, wo, bh, wv


def data_grads(target, plane_xy, whole_xz, whole_yz, ws, b_output):
    xy = jnp.transpose(plane_xy, (1, 0, 2))
    xz = jnp.transpose(whole_xz.reshape(32, NX, NB, 8), (2, 1, 3, 0)).reshape(NB, NX, 256)
    yz = jnp.transpose(whole_yz, (1, 0, 2))
    vm = pl.BlockSpec(memory_space=pltpu.VMEM)
    gxy, gxz, gyz = pl.pallas_call(
        grad_kernel,
        out_shape=[
            jax.ShapeDtypeStruct((NX, 32, 128), F32),
            jax.ShapeDtypeStruct((NB, NX, 256), F32),
            jax.ShapeDtypeStruct((NB * 8, 32, 128), F32),
        ],
        in_specs=[vm] * 9 + [pl.BlockSpec(memory_space=pltpu.SMEM)],
        out_specs=[vm] * 3,
        scratch_shapes=[
            pltpu.VMEM((256, NX * 128), F32),
            pltpu.VMEM((8, 32, NX * 128), F32),
            pltpu.VMEM((8, NX * 128), F32),
        ],
        compiler_params=pltpu.CompilerParams(vmem_limit_bytes=48 * 2**20),
    )(target, xy, xz, yz, *ws, b_output)
    gxy = jnp.transpose(gxy, (1, 0, 2)) / plane_xy
    gxz = jnp.transpose((gxz / xz).reshape(NB, NX, 8, 32), (3, 1, 0, 2)).reshape(32, NX, NB * 8)
    gyz = jnp.transpose(gyz / yz, (1, 0, 2))
    return gxy, gxz, gyz


def adam(plane, first, second, grads, count):
    first = BETA_ONE * first + (1.0 - BETA_ONE) * grads
    second = BETA_TWO * second + (1.0 - BETA_TWO) * grads * grads
    corr_one = 1.0 - BETA_ONE**count
    corr_two = 1.0 - BETA_TWO**count
    plane = plane - LEARN_RATE * (first / corr_one) / (jnp.sqrt(second / corr_two) + EPSILON)
    return (plane, first, second)


def per_device(
    target,
    plane_xy,
    plane_xz,
    plane_yz,
    first_xy,
    first_xz,
    first_yz,
    second_xy,
    second_xz,
    second_yz,
    w_hidden,
    b_hidden,
    w_output,
    b_output,
):
    ws = weights(w_hidden, b_hidden, w_output)
    for iteration in range(STEPS):
        whole_xz = lax.all_gather(plane_xz, "gy", axis=2, tiled=True)
        whole_yz = lax.all_gather(plane_yz, "gx", axis=1, tiled=True)
        grad_xy, term_xz, term_yz = data_grads(
            target, plane_xy, whole_xz, whole_yz, ws, b_output
        )
        grad_xy = grad_xy + smooth(plane_xy)
        grad_xz = lax.psum_scatter(term_xz, "gy", scatter_dimension=2, tiled=True) + smooth(
            plane_xz
        )
        grad_yz = lax.psum_scatter(term_yz, "gx", scatter_dimension=1, tiled=True) + smooth(
            plane_yz
        )
        count = START + iteration + 1
        plane_xy, first_xy, second_xy = adam(plane_xy, first_xy, second_xy, grad_xy, count)
        plane_xz, first_xz, second_xz = adam(plane_xz, first_xz, second_xz, grad_xz, count)
        plane_yz, first_yz, second_yz = adam(plane_yz, first_yz, second_yz, grad_yz, count)
    return (
        plane_xy,
        plane_xz,
        plane_yz,
        first_xy,
        first_xz,
        first_yz,
        second_xy,
        second_xz,
        second_yz,
    )


def solution(mesh):
    return jax.shard_map(
        per_device,
        mesh=mesh,
        in_specs=(
            P("gx", None, "gy"),
            P(None, "gx", "gy"),
            P(None, "gx", "gy"),
            P(None, "gx", "gy"),
            P(None, "gx", "gy"),
            P(None, "gx", "gy"),
            P(None, "gx", "gy"),
            P(None, "gx", "gy"),
            P(None, "gx", "gy"),
            P(None, "gx", "gy"),
            P(),
            P(),
            P(),
            P(),
        ),
        out_specs=(
            P(None, "gx", "gy"),
            P(None, "gx", "gy"),
            P(None, "gx", "gy"),
            P(None, "gx", "gy"),
            P(None, "gx", "gy"),
            P(None, "gx", "gy"),
            P(None, "gx", "gy"),
            P(None, "gx", "gy"),
            P(None, "gx", "gy"),
        ),
        check_vma=False,
    )
```

```python
import functools
import jax
import jax.numpy as jnp
from jax import lax
from jax.experimental import pallas as pl
from jax.experimental.pallas import tpu as pltpu
from jax.sharding import PartitionSpec as P

STEPS = 2
START = 20


BETA_ONE = 0.9
BETA_TWO = 0.99
LEARN_RATE = 0.01
EPSILON = 1e-08
NX = 16
F32 = jnp.float32
BF = jnp.bfloat16
MESH = pl.DeviceIdType.MESH


def grad_block(zb, s, tgt, xy, xz, yz, w1, w2, wo, bh, wv, b0, accxy, gxz, gyz, fbuf, dbuf, rbuf):
    wide = NX * 128
    xt = jnp.transpose(xz[s, zb])
    h1 = xt.astype(BF)
    r1 = xt - h1.astype(F32)
    h2 = r1.astype(BF)
    h3 = (r1 - h2.astype(F32)).astype(BF)
    parts = jnp.concatenate([h1, h2, h3], axis=1)
    place = lax.broadcasted_iota(jnp.int32, (3 * NX, 128), 0) % NX
    yzt = yz[s, pl.ds(zb * 8, 8)].reshape(256, 128)
    for x in range(NX):
        col = jnp.dot(parts, (place == x).astype(BF), preferred_element_type=F32)
        f = ((col * yzt).reshape(8, 32, 128) * xy[x + 1][None]).reshape(256, 128)
        fbuf[:, x * 128 : (x + 1) * 128] = f
    pre = jnp.dot(w1[...], fbuf[...].astype(BF), preferred_element_type=F32)
    q = pre.reshape(8, 32, wide) + jnp.concatenate([bh[...]] * NX, axis=-1)[None]
    u = 1.0 + jnp.tanh(q)
    h = q * u
    dbuf[...] = (u + h * (2.0 - u)) * jnp.concatenate([wv[...]] * NX, axis=-1)[None]
    out = jnp.dot(wo[...], h.reshape(256, wide).astype(BF), preferred_element_type=F32)[:8]
    for x in range(NX):
        rbuf[:, x * 128 : (x + 1) * 128] = (
            out[:, x * 128 : (x + 1) * 128] + b0 - tgt[x, pl.ds(zb * 8, 8), :]
        )
    d = (dbuf[...] * rbuf[...][:, None, :]).reshape(256, wide)
    s = jnp.dot(w2[...], d.astype(BF), preferred_element_type=F32) * fbuf[...]
    acc = None
    for x in range(NX):
        sx = s[:, x * 128 : (x + 1) * 128]
        acc = sx if acc is None else acc + sx
        accxy[x] += jnp.sum(sx.reshape(8, 32, 128), axis=0)
        gxz[zb, x : x + 1, :] = jnp.sum(sx, axis=-1).reshape(1, 256)
    gyz[pl.ds(zb * 8, 8)] = acc.reshape(8, 32, 128)


def weights(w_hidden, b_hidden, w_output):
    eye = jnp.eye(8, dtype=F32)
    wf = w_hidden.astype(F32)
    w1 = jnp.kron(eye, 0.5 * wf.T).astype(BF)
    w2 = jnp.kron(eye, wf).astype(BF)
    wof = w_output.astype(F32)
    wo = jnp.pad(jnp.kron(eye, wof[None, :]), ((0, 8), (0, 0))).astype(BF)
    bh = jnp.broadcast_to((0.5 * b_hidden)[:, None], (32, 128))
    wv = jnp.broadcast_to((0.5 * wof)[:, None], (32, 128))
    return w1, w2, wo, bh, wv


def copy_to(src, dst, send, recv, device):
    return pltpu.make_async_remote_copy(
        src_ref=src,
        dst_ref=dst,
        send_sem=send,
        recv_sem=recv,
        device_id=device,
        device_id_type=MESH,
    )


def adam(plane, first, second, grads, scale_one, scale_two):
    first = BETA_ONE * first + (1.0 - BETA_ONE) * grads
    second = BETA_TWO * second + (1.0 - BETA_TWO) * grads * grads
    plane = plane - LEARN_RATE * (first * scale_one) / (jnp.sqrt(second * scale_two) + EPSILON)
    return (plane, first, second)


def fit_kernel(
    nk,
    nj,
    tgt, xy_in, xz_in, yz_in, mxy_in, mxz_in, myz_in, vxy_in, vxz_in, vyz_in,
    w1, w2, wo, bh, wv, bo,
    xy, xz, yz, mxy, mxz, myz, vxy, vxz, vyz,
    xyp, xza, yza, gxy, gxz, gyz, sib, total, parts, xparts, fbuf, dbuf, rbuf,
    row_out, row_in, col_out, col_in,
    yz_recv, yz_send, relay_send, xz_recv, xz_send, row_recv, row_send, col_recv, col_send,
    sib_recv, sib_send, part_recv, part_send, xpart_recv, xpart_send,
):
    i = lax.axis_index("gx")
    j = lax.axis_index("gy")
    k = i // 2
    core = i % 2
    other = 1 - core
    own = nk // nj
    sibling = (2 * k + other, j)
    b0 = bo[0]
    lane = lax.broadcasted_iota(jnp.int32, (32, 128), 1)

    def chip(offset):
        return (k + offset + nk) % nk

    barrier = pltpu.get_barrier_semaphore()

    def greet(device):
        pl.semaphore_signal(barrier, inc=1, device_id=device, device_id_type=MESH)

    def greet_chip(r, carry):
        greet((2 * chip(r) + core, j))
        return carry

    def greet_column(r, carry):
        greet((i, (j + r) % nj))
        return carry

    greet(sibling)
    greet((2 * chip(1) + other, j))
    greet((2 * chip(-1) + other, j))
    lax.fori_loop(1, nk, greet_chip, 0)
    lax.fori_loop(1, nj, greet_column, 0)

    xyp[pl.ds(1, NX)] = xy_in[...]
    xza[0, pl.ds(j * own, own)] = xz_in[...]
    yza[0, pl.ds(4 * i, 4)] = yz_in[...]
    mxy[...] = mxy_in[...]
    mxz[...] = mxz_in[...]
    myz[...] = myz_in[...]
    vxy[...] = vxy_in[...]
    vxz[...] = vxz_in[...]
    vyz[...] = vyz_in[...]
    pl.semaphore_wait(barrier, nk + nj + 1)

    def yz_copy(s, r, device, slot):
        mine = yza.at[s, pl.ds(4 * i, 4)]
        return copy_to(mine, mine, yz_send.at[slot], yz_recv.at[s, k, core], device)

    def yz_wait(s, chip_index, half):
        part = yza.at[s, pl.ds(8 * chip_index + 4 * half, 4)]
        copy_to(part, part, yz_send.at[0], yz_recv.at[s, chip_index, half], sibling).wait_recv()

    def relay_copy(s, chip_index):
        part = yza.at[s, pl.ds(8 * chip_index + 4 * core, 4)]
        return copy_to(
            part, part, relay_send.at[chip_index], yz_recv.at[s, chip_index, core], sibling
        )

    def xz_copy(s, r):
        mine = xza.at[s, pl.ds(j * own, own)]
        return copy_to(mine, mine, xz_send.at[r], xz_recv.at[s, j], (i, (j + r) % nj))

    def xz_wait(s, r):
        peer = (j + r) % nj
        part = xza.at[s, pl.ds(peer * own, own)]
        copy_to(part, part, xz_send.at[0], xz_recv.at[s, peer], (i, peer)).wait_recv()

    def row_copy(s, side):
        device = ((i + 1) % (2 * nk), j) if side == 0 else ((i + 2 * nk - 1) % (2 * nk), j)
        return copy_to(
            row_out.at[side], row_in.at[s, side], row_send.at[side], row_recv.at[s, side], device
        )

    def col_copy(s, side):
        device = (i, (j + 1) % nj) if side == 0 else (i, (j + nj - 1) % nj)
        return copy_to(
            col_out.at[side], col_in.at[s, side], col_send.at[side], col_recv.at[s, side], device
        )

    def sib_copy(s, chip_index):
        return copy_to(
            gyz.at[pl.ds(8 * chip_index + 4 * other, 4)],
            sib.at[s, chip_index],
            sib_send.at[chip_index],
            sib_recv.at[s, chip_index],
            sibling,
        )

    def part_copy(s, chip_index):
        return copy_to(
            total.at[chip_index],
            parts.at[s, k],
            part_send.at[chip_index],
            part_recv.at[s, k],
            (2 * chip_index + core, j),
        )

    def part_wait(s, r):
        peer = chip(r)
        slot = parts.at[s, peer]
        copy_to(
            slot, slot, part_send.at[0], part_recv.at[s, peer], (2 * peer + core, j)
        ).wait_recv()

    def xpart_copy(s, zb):
        return copy_to(
            gxz.at[zb],
            xparts.at[s, j, zb % own],
            xpart_send.at[zb],
            xpart_recv.at[s, j, zb % own],
            (i, zb // own),
        )

    def xpart_wait(s, peer, n):
        slot = xparts.at[s, peer, n]
        copy_to(
            slot, slot, xpart_send.at[0], xpart_recv.at[s, peer, n], (i, peer)
        ).wait_recv()

    def loop(low, high, body):
        def step(r, carry):
            body(r)
            return carry

        lax.fori_loop(low, high, step, 0)

    def send_yz(s):
        yz_copy(s, 0, sibling, 0).start()
        yz_copy(s, 1, (2 * chip(-1) + core, j), 1).start()
        yz_copy(s, 1, (2 * chip(-1) + other, j), nk).start()
        loop(2, nk, lambda r: yz_copy(s, r, (2 * chip(-r) + core, j), r).start())

    def send_xz(s):
        loop(1, nj, lambda r: xz_copy(s, r).start())

    def send_borders(s):
        for side, x in ((0, NX - 1), (1, 0)):
            row_out[side, pl.ds(0, 32)] = xyp[x + 1]
            line = xza[s, pl.ds(j * own, own), x, :]
            row_out[side, pl.ds(32, own)] = line[:, :128]
            row_out[side, pl.ds(32 + own, own)] = line[:, 128:]
            row_copy(s, side).start()
        for side, last in ((0, 127), (1, 0)):
            cols = jnp.zeros((32, 128), F32)
            for n in range(NX + 4):
                piece = xyp[n + 1] if n < NX else yza[s, 4 * i + n - NX]
                cols = jnp.where(lane == n, pltpu.roll(piece, (n - last + 128) % 128, 1), cols)
            col_out[side] = cols
            col_copy(s, side).start()

    def finish_block(s, t):
        kp = chip(t)
        copy_to(
            sib.at[s, kp], sib.at[s, kp], sib_send.at[0], sib_recv.at[s, kp], sibling
        ).wait_recv()
        both = gyz[pl.ds(8 * kp + 4 * core, 4)] + sib[s, kp]

        @pl.when(t == 0)
        def _():
            parts[s, k] = both

        @pl.when(t > 0)
        def _():
            total[kp] = both
            part_copy(s, kp).start()

    def one_step(s):
        gxy[...] = jnp.zeros_like(gxy)
        loop(1, nj, lambda r: xz_wait(s, r))

        def block(t):
            kk = chip(t)
            yz_wait(s, kk, other)

            @pl.when(t == 1)
            def _():
                yz_wait(s, kk, core)

            grad_block(
                kk, s, tgt, xyp, xza, yza, w1, w2, wo, bh, wv, b0, gxy, gxz, gyz, fbuf, dbuf, rbuf
            )
            sib_copy(s, kk).start()
            keep = kk // own == j

            @pl.when(keep)
            def _():
                xparts[s, j, kk % own] = gxz[kk]

            @pl.when(jnp.logical_not(keep))
            def _():
                xpart_copy(s, kk).start()

            @pl.when(t + 2 < nk)
            def _():
                ahead = chip(t + 2)
                yz_wait(s, ahead, core)
                relay_copy(s, ahead).start()

            @pl.when(t >= 1)
            def _():
                finish_block(s, t - 1)

        loop(0, nk, block)
        finish_block(s, nk - 1)

        scale_one = jnp.where(s == 0, *(1.0 / (1.0 - BETA_ONE ** (START + n)) for n in (1, 2)))
        scale_two = jnp.where(s == 0, *(1.0 / (1.0 - BETA_TWO ** (START + n)) for n in (1, 2)))

        for side in range(2):
            row_copy(s, side).wait_recv()
            col_copy(s, side).wait_recv()
        xyp[0] = jnp.where(i == 0, xyp[1], row_in[s, 0, pl.ds(0, 32)])
        xyp[NX + 1] = jnp.where(i == 2 * nk - 1, xyp[NX], row_in[s, 1, pl.ds(0, 32)])
        before = col_in[s, 0]
        after = col_in[s, 1]

        def sides(plane, n):
            left = jnp.where(j == 0, plane, pltpu.roll(before, 128 - n, 1))
            left = jnp.where(lane == 0, left, pltpu.roll(plane, 1, 1))
            right = jnp.where(j == nj - 1, plane, pltpu.roll(after, 127 - n, 1))
            right = jnp.where(lane == 127, right, pltpu.roll(plane, 127, 1))
            return left + right

        def update_xy(x):
            plane = xyp[x + 1]
            rough = 4.0 * plane - xyp[x] - xyp[x + 2] - sides(plane, x)
            grads = gxy[x] / plane + rough
            xy[x], mxy[x], vxy[x] = adam(plane, mxy[x], vxy[x], grads, scale_one, scale_two)

        loop(0, NX, update_xy)

        for r in range(1, nj):
            for n in range(own):
                xpart_wait(s, (j + r) % nj, n)
        lane_xz = lax.broadcasted_iota(jnp.int32, (NX, 256), 1)
        spot_xz = lax.broadcasted_iota(jnp.int32, (NX, 256), 0)
        for n in range(own):
            zb = j * own + n
            plane = xza[s, zb]
            line = [
                jnp.concatenate(
                    [row_in[s, side, 32 + n : 33 + n], row_in[s, side, 32 + own + n : 33 + own + n]],
                    axis=1,
                )
                for side in range(2)
            ]
            up = jnp.where(i == 0, plane, jnp.broadcast_to(line[0], plane.shape))
            up = jnp.where(spot_xz == 0, up, pltpu.roll(plane, 1, 0))
            down = jnp.where(i == 2 * nk - 1, plane, jnp.broadcast_to(line[1], plane.shape))
            down = jnp.where(spot_xz == NX - 1, down, pltpu.roll(plane, NX - 1, 0))
            low = pltpu.roll(xza[s, jnp.maximum(zb - 1, 0)], 32, 1)
            low = jnp.where(zb == 0, plane, low)
            low = jnp.where(lane_xz < 32, low, pltpu.roll(plane, 32, 1))
            high = pltpu.roll(xza[s, jnp.minimum(zb + 1, nk - 1)], 224, 1)
            high = jnp.where(zb == nk - 1, plane, high)
            high = jnp.where(lane_xz >= 224, high, pltpu.roll(plane, 224, 1))
            term = xparts[s, 0, n]
            for peer in range(1, nj):
                term = term + xparts[s, peer, n]
            grads = term / plane + (4.0 * plane - up - down - low - high)
            xz[n], mxz[n], vxz[n] = adam(plane, mxz[n], vxz[n], grads, scale_one, scale_two)

        @pl.when(s + 1 < STEPS)
        def _():
            xza[1, pl.ds(j * own, own)] = xz[...]
            send_later(loop_xz_sent, send_xz)

        loop(1, nk, lambda r: part_wait(s, r))
        for n in range(4):
            z = 4 * i + n
            plane = yza[s, z]
            low = yza[s, jnp.maximum(z - 1, 0)]
            high = yza[s, jnp.minimum(z + 1, 8 * nk - 1)]
            rough = 4.0 * plane - low - high - sides(plane, NX + n)
            term = parts[s, 0, n]
            for peer in range(1, nk):
                term = term + parts[s, peer, n]
            grads = term / plane + rough
            yz[n], myz[n], vyz[n] = adam(plane, myz[n], vyz[n], grads, scale_one, scale_two)

        @pl.when(s + 1 < STEPS)
        def _():
            yza[1, pl.ds(4 * i, 4)] = yz[...]
            loop_yz_sent()
            send_yz(1)
            xyp[pl.ds(1, NX)] = xy[...]

        sent()

        @pl.when(s + 1 < STEPS)
        def _():
            send_borders(1)

    def loop_yz_sent():
        for slot in range(nk + 1):
            yz_copy(0, 0, sibling, slot).wait_send()

    def loop_xz_sent():
        loop(1, nj, lambda r: xz_copy(0, r).wait_send())

    def send_later(first, then):
        first()
        then(1)

    def sent():
        for side in range(2):
            row_copy(0, side).wait_send()
            col_copy(0, side).wait_send()
        loop(2, nk, lambda t: relay_copy(0, chip(t)).wait_send())
        loop(0, nk, lambda t: sib_copy(0, chip(t)).wait_send())
        loop(1, nk, lambda t: part_copy(0, chip(t)).wait_send())

        def xpart_sent(zb):
            @pl.when(zb // own != j)
            def _():
                xpart_copy(0, zb).wait_send()

        loop(0, nk, xpart_sent)

    send_yz(0)
    send_xz(0)
    send_borders(0)
    loop(0, STEPS, one_step)
    loop_yz_sent()
    loop_xz_sent()


def per_device(
    nk,
    nj,
    target,
    plane_xy,
    plane_xz,
    plane_yz,
    first_xy,
    first_xz,
    first_yz,
    second_xy,
    second_xz,
    second_yz,
    w_hidden,
    b_hidden,
    w_output,
    b_output,
):
    own = nk // nj

    def swap(a):
        return jnp.transpose(a, (1, 0, 2))

    def pack(a):
        return jnp.transpose(a.reshape(32, NX, own, 8), (2, 1, 3, 0)).reshape(own, NX, 256)

    def unpack(a):
        return jnp.transpose(a.reshape(own, NX, 8, 32), (3, 1, 0, 2)).reshape(32, NX, own * 8)

    vm = pl.BlockSpec(memory_space=pltpu.VMEM)
    shapes = [(NX, 32, 128), (own, NX, 256), (4, 32, 128)] * 3
    dma = pltpu.SemaphoreType.DMA
    outs = pl.pallas_call(
        functools.partial(fit_kernel, nk, nj),
        out_shape=[jax.ShapeDtypeStruct(shape, F32) for shape in shapes],
        in_specs=[vm] * 15 + [pl.BlockSpec(memory_space=pltpu.SMEM)],
        out_specs=[vm] * 9,
        scratch_shapes=[
            pltpu.VMEM((NX + 2, 32, 128), F32),
            pltpu.VMEM((2, nk, NX, 256), F32),
            pltpu.VMEM((2, 8 * nk, 32, 128), F32),
            pltpu.VMEM((NX, 32, 128), F32),
            pltpu.VMEM((nk, NX, 256), F32),
            pltpu.VMEM((8 * nk, 32, 128), F32),
            pltpu.VMEM((2, nk, 4, 32, 128), F32),
            pltpu.VMEM((nk, 4, 32, 128), F32),
            pltpu.VMEM((2, nk, 4, 32, 128), F32),
            pltpu.VMEM((2, nj, own, NX, 256), F32),
            pltpu.VMEM((256, NX * 128), F32),
            pltpu.VMEM((8, 32, NX * 128), F32),
            pltpu.VMEM((8, NX * 128), F32),
            pltpu.VMEM((2, 40, 128), F32),
            pltpu.VMEM((2, 2, 40, 128), F32),
            pltpu.VMEM((2, 32, 128), F32),
            pltpu.VMEM((2, 2, 32, 128), F32),
            dma((2, nk, 2)),
            dma((nk + 1,)),
            dma((nk,)),
            dma((2, nj)),
            dma((nj,)),
            dma((2, 2)),
            dma((2,)),
            dma((2, 2)),
            dma((2,)),
            dma((2, nk)),
            dma((nk,)),
            dma((2, nk)),
            dma((nk,)),
            dma((2, nj, own)),
            dma((nk,)),
        ],
        compiler_params=pltpu.CompilerParams(
            collective_id=0, has_side_effects=True, vmem_limit_bytes=56 * 2**20
        ),
    )(
        target,
        swap(plane_xy),
        pack(plane_xz),
        swap(plane_yz),
        swap(first_xy),
        pack(first_xz),
        swap(first_yz),
        swap(second_xy),
        pack(second_xz),
        swap(second_yz),
        *weights(w_hidden, b_hidden, w_output),
        b_output,
    )
    return tuple(unpack(a) if n % 3 == 1 else swap(a) for n, a in enumerate(outs))


def solution(mesh):
    piece = P(None, "gx", "gy")
    return jax.shard_map(
        functools.partial(per_device, mesh.shape["gx"] // 2, mesh.shape["gy"]),
        mesh=mesh,
        in_specs=(P("gx", None, "gy"),) + (piece,) * 9 + (P(),) * 4,
        out_specs=(piece,) * 9,
        check_vma=False,
    )
```

```python
import functools
import jax
import jax.numpy as jnp
from jax import lax
from jax.experimental import pallas as pl
from jax.experimental.pallas import tpu as pltpu
from jax.sharding import PartitionSpec as P

STEPS = 2
START = 20


BETA_ONE = 0.9
BETA_TWO = 0.99
LEARN_RATE = 0.01
EPSILON = 1e-08
NX = 16
F32 = jnp.float32
BF = jnp.bfloat16
MESH = pl.DeviceIdType.MESH


def grad_block(
    u, low_chip, high_chip, s, tgt, xy, xz, yz, w1, w2, wo, bh, wv, b0, gxy, gxz, gyz, fbuf, dbuf, rbuf
):
    wide = NX * 128
    xt = jnp.transpose(
        jnp.concatenate([xz[s, low_chip][:, :128], xz[s, high_chip][:, 128:]], axis=1)
    )
    h1 = xt.astype(BF)
    r1 = xt - h1.astype(F32)
    h2 = r1.astype(BF)
    h3 = (r1 - h2.astype(F32)).astype(BF)
    parts = jnp.concatenate([h1, h2, h3], axis=1)
    place = lax.broadcasted_iota(jnp.int32, (3 * NX, 128), 0) % NX
    yzt = jnp.concatenate(
        [yz[s, pl.ds(8 * low_chip, 4)], yz[s, pl.ds(8 * high_chip + 4, 4)]], axis=0
    ).reshape(256, 128)
    for x in range(NX):
        col = jnp.dot(parts, (place == x).astype(BF), preferred_element_type=F32)
        f = ((col * yzt).reshape(8, 32, 128) * xy[x + 1][None]).reshape(256, 128)
        fbuf[:, x * 128 : (x + 1) * 128] = f
    pre = jnp.dot(w1[...], fbuf[...].astype(BF), preferred_element_type=F32)
    q = pre.reshape(8, 32, wide) + jnp.concatenate([bh[...]] * NX, axis=-1)[None]
    t = 1.0 + jnp.tanh(q)
    h = q * t
    dbuf[...] = (t + h * (2.0 - t)) * jnp.concatenate([wv[...]] * NX, axis=-1)[None]
    out = jnp.dot(wo[...], h.reshape(256, wide).astype(BF), preferred_element_type=F32)[:8]
    low = lax.broadcasted_iota(jnp.int32, (8, 128), 0) < 4
    for x in range(NX):
        want = jnp.where(low, tgt[x, pl.ds(8 * low_chip, 8), :], tgt[x, pl.ds(8 * high_chip, 8), :])
        rbuf[:, x * 128 : (x + 1) * 128] = out[:, x * 128 : (x + 1) * 128] + b0 - want
    d = (dbuf[...] * rbuf[...][:, None, :]).reshape(256, wide)
    p = jnp.dot(w2[...], d.astype(BF), preferred_element_type=F32) * fbuf[...]
    acc = None
    for x in range(NX):
        px = p[:, x * 128 : (x + 1) * 128]
        acc = px if acc is None else acc + px
        gxy[x] += jnp.sum(px.reshape(8, 32, 128), axis=0)
        row = jnp.sum(px, axis=-1).reshape(1, 256)
        gxz[low_chip, 0, x : x + 1, :] = row[:, :128]
        gxz[high_chip, 1, x : x + 1, :] = row[:, 128:]
    gyz[u] = acc.reshape(2, 4, 32, 128)


def copy_to(src, dst, send, recv, device):
    return pltpu.make_async_remote_copy(
        src_ref=src,
        dst_ref=dst,
        send_sem=send,
        recv_sem=recv,
        device_id=device,
        device_id_type=MESH,
    )


def adam(plane, first, second, grads, scale_one, scale_two):
    first = BETA_ONE * first + (1.0 - BETA_ONE) * grads
    second = BETA_TWO * second + (1.0 - BETA_TWO) * grads * grads
    plane = plane - LEARN_RATE * (first * scale_one) / (jnp.sqrt(second * scale_two) + EPSILON)
    return (plane, first, second)


def scales(step):
    return (1.0 / (1.0 - BETA_ONE ** (START + 1 + step)), 1.0 / (1.0 - BETA_TWO ** (START + 1 + step)))


def fit_kernel(
    nk,
    nj,
    tgt, xy_in, xz_in, yz_in, mxy_in, mxz_in, myz_in, vxy_in, vxz_in, vyz_in, w_hidden, small,
    xy_out, mxy_out, vxy_out, gxy_out, yz_out, myz_out, vyz_out, gyz_out, xz_out, mxz_out, vxz_out, gxz_out,
    xyp, mxy, vxy, mxz, vxz, gradxz, myz, vyz, xza, yza, gxy, gxz, gyz, sib, total, chain, saved, ypart, xparts,
    fbuf, dbuf, rbuf, row_out, row_in, col_out, col_in, w1, w2, wo, bh, wv,
    load, store,
    yz_recv, yz_send, relay_send, pass_send, xz_recv, xz_send, row_recv, row_send, col_recv, col_send,
    sib_recv, sib_send, chain_recv, chain_send, ypart_recv, ypart_send, xpart_recv, xpart_send,
):
    i = lax.axis_index("gx")
    j = lax.axis_index("gy")
    nz = nk // 2
    tiles = 2 * nz
    k = i // 2
    core = i % 2
    other = 1 - core
    high = k // nz
    zc = k % nz
    toward = 1 - 2 * core
    own = nk // nj
    sibling = (2 * k + other, j)
    following = (2 * (high * nz + (zc + toward + nz) % nz) + core, j)
    preceding = (2 * (high * nz + (zc - toward + nz) % nz) + core, j)
    partner = (2 * ((1 - high) * nz + zc) + core, j)
    partner_other = (2 * ((1 - high) * nz + zc) + other, j)

    def near(plane, offset, c):
        return (2 * (plane * nz + (zc + offset + nz) % nz) + c, j)

    after_row = ((i + 1) % (2 * nk), j)
    before_row = ((i + 2 * nk - 1) % (2 * nk), j)
    border = (2 * ((k + toward * (-1) + nk) % nk) + other, j)
    b0 = small[:, 64:65]
    b_hidden = small[:, :32]
    w_output = small[:, 32:64]
    lane = lax.broadcasted_iota(jnp.int32, (32, 128), 1)

    def loop(low, top, body):
        def step(r, carry):
            body(r)
            return carry

        lax.fori_loop(low, top, step, 0)

    def load_rows(src, dst, first, count, n):
        loop(0, count, lambda r: pltpu.make_async_copy(src.at[:, r, :], dst.at[first + r], load.at[n]).start())

    def loaded(dst, first, count, n):
        whole = dst.at[pl.ds(first, count)]
        pltpu.make_async_copy(whole, whole, load.at[n]).wait()

    def store_rows(src, first, dst, count, n):
        loop(0, count, lambda r: pltpu.make_async_copy(src.at[first + r], dst.at[:, r, :], store.at[n]).start())

    def stored(src, first, count, n):
        whole = src.at[pl.ds(first, count)]
        pltpu.make_async_copy(whole, whole, store.at[n]).wait()

    mine_yz = yza.at[0, pl.ds(4 * i, 4)]
    loop(0, 4, lambda r: pltpu.make_async_copy(yz_in.at[:, r, :], yza.at[0, 4 * i + r], load.at[1]).start())
    load_rows(xy_in, xyp, 1, NX, 0)
    load_rows(mxy_in, mxy, 0, NX, 2)
    load_rows(vxy_in, vxy, 0, NX, 3)
    load_rows(myz_in, myz, 0, 4, 4)
    load_rows(vyz_in, vyz, 0, 4, 5)

    barrier = pltpu.get_barrier_semaphore()

    def greet(device):
        pl.semaphore_signal(barrier, inc=1, device_id=device, device_id_type=MESH)

    targets = [sibling, partner, partner_other]
    for plane in (high, 1 - high):
        for c in (core, other):
            targets.append(near(plane, toward, c))
    for device in targets:
        greet(device)
    for device in (near(high, -toward, core), near(1 - high, -toward, core), border):
        greet(device)
    loop(1, nj, lambda r: greet((i, (j + r) % nj)))

    def gathered(src, n):
        return jnp.concatenate([src[:, 8 * n + z, :] for z in range(8)], axis=1)

    def spread(dst, n, values):
        for z in range(8):
            dst[:, 8 * n + z, :] = values[:, 32 * z : 32 * z + 32]

    for n in range(own):
        xza[0, j * own + n] = gathered(xz_in, n)
        mxz[n] = gathered(mxz_in, n)
        vxz[n] = gathered(vxz_in, n)

    def tile(u):
        t = (u // 2 + 1) % nz
        e = (u % 2 + jnp.where(t == 0, 1, 0)) % 2
        base = ((high + e) % 2) * nz
        return t, e, base + (zc - t + nz) % nz, base + (zc + t) % nz

    def my_chip(u):
        _, _, low_chip, high_chip = tile(u)
        return jnp.where(core == 0, low_chip, high_chip)

    def other_chip(u):
        _, _, low_chip, high_chip = tile(u)
        return jnp.where(core == 0, high_chip, low_chip)

    def yz_copy(s, device, slot):
        mine = yza.at[s, pl.ds(4 * i, 4)]
        return copy_to(mine, mine, yz_send.at[slot], yz_recv.at[s, k, core], device)

    def yz_wait(s, chip, half):
        part = yza.at[s, pl.ds(8 * chip + 4 * half, 4)]
        copy_to(part, part, yz_send.at[0], yz_recv.at[s, chip, half], sibling).wait_recv()

    def relay_copy(s, u):
        chip = my_chip(u)
        part = yza.at[s, pl.ds(8 * chip + 4 * core, 4)]
        return copy_to(part, part, relay_send.at[u], yz_recv.at[s, chip, core], sibling)

    def pass_copy(s, u):
        chip = my_chip(u)
        part = yza.at[s, pl.ds(8 * chip + 4 * core, 4)]
        return copy_to(part, part, pass_send.at[u], yz_recv.at[s, chip, core], following)

    def xz_copy(s, r):
        mine = xza.at[s, pl.ds(j * own, own)]
        return copy_to(mine, mine, xz_send.at[r], xz_recv.at[s, j], (i, (j + r) % nj))

    def xz_wait(s, r):
        peer = (j + r) % nj
        part = xza.at[s, pl.ds(peer * own, own)]
        copy_to(part, part, xz_send.at[0], xz_recv.at[s, peer], (i, peer)).wait_recv()

    def row_copy(s, side):
        return copy_to(
            row_out.at[side],
            row_in.at[s, side],
            row_send.at[side],
            row_recv.at[s, side],
            after_row if side == 0 else before_row,
        )

    def col_copy(s, side):
        device = (i, (j + 1) % nj) if side == 0 else (i, (j + nj - 1) % nj)
        return copy_to(
            col_out.at[side], col_in.at[s, side], col_send.at[side], col_recv.at[s, side], device
        )

    def sib_copy(s, u):
        return copy_to(gyz.at[u, other], sib.at[s, u], sib_send.at[u], sib_recv.at[s, u], sibling)

    def chain_copy(s, u, slot):
        return copy_to(
            total.at[u], chain.at[s, slot], chain_send.at[u], chain_recv.at[s, slot], following
        )

    def chain_wait(s, slot):
        part = chain.at[s, slot]
        copy_to(part, part, chain_send.at[0], chain_recv.at[s, slot], following).wait_recv()

    def ypart_copy(s):
        return copy_to(saved.at[1], ypart.at[s], ypart_send, ypart_recv.at[s], partner)

    def xpart_copy(s, chip, half):
        slot = 2 * (chip % own) + half
        return copy_to(
            gxz.at[chip, half],
            xparts.at[s, j, slot],
            xpart_send.at[chip, half],
            xpart_recv.at[s, j, slot],
            (i, chip // own),
        )

    def xpart_wait(s, peer, n):
        slot = xparts.at[s, peer, n]
        copy_to(
            slot, slot, xpart_send.at[0, 0], xpart_recv.at[s, peer, n], (i, peer)
        ).wait_recv()

    def send_yz(s):
        for slot in (3, 4, 5, 6, 0, 1, 2):
            yz_copy(s, targets[slot], slot).start()

    def yz_sent():
        for slot in range(7):
            yz_copy(0, sibling, slot).wait_send()
        loop(0, tiles - 4, lambda u: pass_copy(0, u).wait_send())
        loop(2, tiles - 2, lambda u: relay_copy(0, u).wait_send())

    def send_xz(s):
        loop(1, nj, lambda r: xz_copy(s, r).start())

    def xz_sent():
        loop(1, nj, lambda r: xz_copy(0, r).wait_send())

    def send_borders(s):
        for side, x in ((0, NX - 1), (1, 0)):
            row_out[side, pl.ds(0, 32)] = xyp[x + 1]
            line = xza[s, pl.ds(j * own, own), x, :]
            row_out[side, pl.ds(32, own)] = line[:, :128]
            row_out[side, pl.ds(32 + own, own)] = line[:, 128:]
            row_copy(s, side).start()
        for side, last in ((0, 127), (1, 0)):
            cols = jnp.zeros((32, 128), F32)
            for n in range(NX + 4):
                piece = xyp[n + 1] if n < NX else yza[s, 4 * i + n - NX]
                cols = jnp.where(lane == n, pltpu.roll(piece, (n - last + 128) % 128, 1), cols)
            col_out[side] = cols
            col_copy(s, side).start()

    def finish_tile(s, u):
        t, e, _, _ = tile(u)
        part = sib.at[s, u]
        copy_to(part, part, sib_send.at[0], sib_recv.at[s, u], sibling).wait_recv()
        both = gyz[u, core] + sib[s, u]

        @pl.when(t == 0)
        def _():
            saved[e] = both

        @pl.when(t == 1)
        def _():
            total[u] = both

        @pl.when(t >= 2)
        def _():
            chain_wait(s, u)
            total[u] = both + chain[s, u]

        @pl.when(t > 0)
        def _():
            chain_copy(s, u, jnp.where(t == nz - 1, tiles + e, u + 2)).start()

    def sent():
        for side in range(2):
            row_copy(0, side).wait_send()
            col_copy(0, side).wait_send()
        loop(0, tiles, lambda u: sib_copy(0, u).wait_send())
        loop(0, tiles - 2, lambda u: chain_copy(0, u, u).wait_send())
        ypart_copy(0).wait_send()

        def xpart_sent(chip):
            @pl.when(chip // own != j)
            def _():
                for half in range(2):
                    xpart_copy(0, chip, half).wait_send()

        loop(0, nk, xpart_sent)

    def one_step(s):
        gxy[...] = jnp.zeros_like(gxy)
        for u in range(2):
            yz_wait(s, my_chip(u), core)

            @pl.when(u + 4 < tiles)
            def _():
                pass_copy(s, u).start()

        loop(1, nj, lambda r: xz_wait(s, r))

        def block(u):
            _, _, low_chip, high_chip = tile(u)
            yz_wait(s, other_chip(u), other)
            grad_block(
                u, low_chip, high_chip, s, tgt, xyp, xza, yza, w1, w2, wo, bh, wv, b0, gxy, gxz, gyz,
                fbuf, dbuf, rbuf,
            )
            sib_copy(s, u).start()
            for half, chip in ((0, low_chip), (1, high_chip)):
                keep = chip // own == j

                @pl.when(keep)
                def _():
                    xparts[s, j, 2 * (chip % own) + half] = gxz[chip, half]

                @pl.when(jnp.logical_not(keep))
                def _():
                    xpart_copy(s, chip, half).start()

            @pl.when(u + 4 < tiles)
            def _():
                yz_wait(s, my_chip(u + 2), core)
                relay_copy(s, u + 2).start()

            @pl.when(u + 6 < tiles)
            def _():
                pass_copy(s, u + 2).start()

            @pl.when(u == tiles - 4)
            def _():
                yz_wait(s, my_chip(tiles - 2), core)

            @pl.when(u >= 1)
            def _():
                finish_tile(s, u - 1)

        loop(0, tiles, block)

        scale_one = jnp.where(s == 0, scales(0)[0], scales(1)[0])
        scale_two = jnp.where(s == 0, scales(0)[1], scales(1)[1])

        for side in range(2):
            row_copy(s, side).wait_recv()
            col_copy(s, side).wait_recv()
        chain_wait(s, tiles + 1)
        saved[1] += chain[s, tiles + 1]
        ypart_copy(s).start()

        before = col_in[s, 0]
        after = col_in[s, 1]

        def sides(plane, n):
            left = jnp.where(j == 0, plane, pltpu.roll(before, 128 - n, 1))
            left = jnp.where(lane == 0, left, pltpu.roll(plane, 1, 1))
            right = jnp.where(j == nj - 1, plane, pltpu.roll(after, 127 - n, 1))
            right = jnp.where(lane == 127, right, pltpu.roll(plane, 127, 1))
            return left + right

        xyp[0] = jnp.where(i == 0, xyp[1], row_in[s, 0, pl.ds(0, 32)])
        xyp[NX + 1] = jnp.where(i == 2 * nk - 1, xyp[NX], row_in[s, 1, pl.ds(0, 32)])

        def update_xy(x):
            plane = xyp[x + 1]
            rough = 4.0 * plane - xyp[x] - xyp[x + 2] - sides(plane, x)
            gxy[x] = gxy[x] / plane + rough

        loop(0, NX, update_xy)

        @pl.when(s == 1)
        def _():
            store_rows(gxy, 0, gxy_out, NX, 6)

        for r in range(1, nj):
            for n in range(2 * own):
                xpart_wait(s, (j + r) % nj, n)
        lane_xz = lax.broadcasted_iota(jnp.int32, (NX, 256), 1)
        spot_xz = lax.broadcasted_iota(jnp.int32, (NX, 256), 0)
        for n in range(own):
            zb = j * own + n
            plane = xza[s, zb]
            line = [
                jnp.concatenate(
                    [row_in[s, side, 32 + n : 33 + n], row_in[s, side, 32 + own + n : 33 + own + n]],
                    axis=1,
                )
                for side in range(2)
            ]
            up = jnp.where(i == 0, plane, jnp.broadcast_to(line[0], plane.shape))
            up = jnp.where(spot_xz == 0, up, pltpu.roll(plane, 1, 0))
            down = jnp.where(i == 2 * nk - 1, plane, jnp.broadcast_to(line[1], plane.shape))
            down = jnp.where(spot_xz == NX - 1, down, pltpu.roll(plane, NX - 1, 0))
            left = pltpu.roll(xza[s, jnp.maximum(zb - 1, 0)], 32, 1)
            left = jnp.where(zb == 0, plane, left)
            left = jnp.where(lane_xz < 32, left, pltpu.roll(plane, 32, 1))
            right = pltpu.roll(xza[s, jnp.minimum(zb + 1, nk - 1)], 224, 1)
            right = jnp.where(zb == nk - 1, plane, right)
            right = jnp.where(lane_xz >= 224, right, pltpu.roll(plane, 224, 1))
            terms = [
                jnp.concatenate([xparts[s, peer, 2 * n], xparts[s, peer, 2 * n + 1]], axis=1)
                for peer in range(nj)
            ]
            grads = sum(terms) / plane + (4.0 * plane - up - down - left - right)
            gradxz[n] = grads

        @pl.when(s == 0)
        def _():
            for n in range(own):
                plane, mxz[n], vxz[n] = adam(
                    xza[0, j * own + n], mxz[n], vxz[n], gradxz[n], scale_one, scale_two
                )
                xza[1, j * own + n] = plane
            xz_sent()
            send_xz(1)

        def update_yz():
            finish_tile(s, tiles - 1)
            chain_wait(s, tiles)
            copy_to(ypart.at[s], ypart.at[s], ypart_send, ypart_recv.at[s], partner).wait_recv()
            for n in range(4):
                z = 4 * i + n
                plane = yza[s, z]
                left = yza[s, jnp.maximum(z - 1, 0)]
                right = yza[s, jnp.minimum(z + 1, 8 * nk - 1)]
                rough = 4.0 * plane - left - right - sides(plane, NX + n)
                saved[0, n] = (saved[0, n] + chain[s, tiles, n] + ypart[s, n]) / plane + rough

        @pl.when(s == 0)
        def _():
            loaded(myz, 0, 4, 4)
            loaded(vyz, 0, 4, 5)
            update_yz()
            for n in range(4):
                yza[1, 4 * i + n], myz[n], vyz[n] = adam(
                    yza[0, 4 * i + n], myz[n], vyz[n], saved[0, n], scale_one, scale_two
                )
            yz_sent()
            send_yz(1)
            loaded(mxy, 0, NX, 2)
            loaded(vxy, 0, NX, 3)
            def step_xy(x):
                xyp[x + 1], mxy[x], vxy[x] = adam(
                    xyp[x + 1], mxy[x], vxy[x], gxy[x], scale_one, scale_two
                )

            loop(0, NX, step_xy)
            sent()
            send_borders(1)
            loop(
                0,
                4,
                lambda r: pltpu.make_async_copy(
                    yza.at[1, 4 * i + r], yz_out.at[:, r, :], store.at[0]
                ).start(),
            )
            store_rows(myz, 0, myz_out, 4, 1)
            store_rows(vyz, 0, vyz_out, 4, 2)
            store_rows(xyp, 1, xy_out, NX, 3)
            store_rows(mxy, 0, mxy_out, NX, 4)
            store_rows(vxy, 0, vxy_out, NX, 5)

        @pl.when(s == 1)
        def _():
            for n in range(own):
                spread(xz_out, n, xza[1, j * own + n])
                spread(mxz_out, n, mxz[n])
                spread(vxz_out, n, vxz[n])
                spread(gxz_out, n, gradxz[n])
            update_yz()
            loop(
                0,
                4,
                lambda r: pltpu.make_async_copy(
                    saved.at[0, r], gyz_out.at[:, r, :], store.at[7]
                ).start(),
            )

    wide = w_hidden[...].astype(F32)
    turned = lax.dot_general(
        w_hidden[...],
        (lax.broadcasted_iota(jnp.int32, (32, 32), 0) == lax.broadcasted_iota(jnp.int32, (32, 32), 1)).astype(BF),
        (((0,), (0,)), ((), ())),
        preferred_element_type=F32,
    )
    same = (
        lax.broadcasted_iota(jnp.int32, (256, 256), 0) // 32
        == lax.broadcasted_iota(jnp.int32, (256, 256), 1) // 32
    )

    def blocks(a):
        a = jnp.concatenate([a] * 8, axis=1)
        return jnp.where(same, jnp.concatenate([a] * 8, axis=0), 0.0).astype(BF)

    w1[...] = blocks(0.5 * turned)
    w2[...] = blocks(wide)
    line_out = jnp.broadcast_to(jnp.concatenate([w_output] * 8, axis=1), (16, 256))
    wo[...] = jnp.where(
        lax.broadcasted_iota(jnp.int32, (16, 256), 0)
        == lax.broadcasted_iota(jnp.int32, (16, 256), 1) // 32,
        line_out,
        0.0,
    ).astype(BF)
    square = lax.broadcasted_iota(jnp.int32, (32, 32), 0) == lax.broadcasted_iota(jnp.int32, (32, 32), 1)

    def column(row):
        kept = jnp.where(square, jnp.broadcast_to(row, (32, 32)), 0.0)
        return jnp.broadcast_to(jnp.sum(kept, axis=1, keepdims=True), (32, 128))

    bh[...] = column(0.5 * b_hidden)
    wv[...] = column(0.5 * w_output)

    whole = yza.at[0, pl.ds(4 * i, 4)]
    pltpu.make_async_copy(whole, whole, load.at[1]).wait()
    pl.semaphore_wait(barrier, nj + 9)
    send_yz(0)
    send_xz(0)
    loaded(xyp, 1, NX, 0)
    send_borders(0)
    loop(0, STEPS, one_step)
    sent()
    xz_sent()
    yz_sent()
    whole_one = yza.at[1, pl.ds(4 * i, 4)]
    pltpu.make_async_copy(whole_one, whole_one, store.at[0]).wait()
    stored(myz, 0, 4, 1)
    stored(vyz, 0, 4, 2)
    stored(xyp, 1, NX, 3)
    stored(mxy, 0, NX, 4)
    stored(vxy, 0, NX, 5)
    stored(gxy, 0, NX, 6)
    pltpu.make_async_copy(saved.at[0], saved.at[0], store.at[7]).wait()


def per_device(
    nk,
    nj,
    target,
    plane_xy,
    plane_xz,
    plane_yz,
    first_xy,
    first_xz,
    first_yz,
    second_xy,
    second_xz,
    second_yz,
    w_hidden,
    b_hidden,
    w_output,
    b_output,
):
    own = nk // nj

    def turn(a):
        return jnp.transpose(a, (1, 2, 0))

    vm = pl.BlockSpec(memory_space=pltpu.VMEM)
    far = pl.BlockSpec(memory_space=pl.ANY)
    dma = pltpu.SemaphoreType.DMA
    tiles = nk
    block = (4, 32, 128)
    shapes = [(32, NX, 128)] * 4 + [(32, 4, 128)] * 4 + [(NX, 8 * own, 32)] * 4
    outs = pl.pallas_call(
        functools.partial(fit_kernel, nk, nj),
        out_shape=[jax.ShapeDtypeStruct(shape, F32) for shape in shapes],
        in_specs=[vm, far, vm, far, far, vm, far, far, vm, far, vm, vm],
        out_specs=[far] * 8 + [vm] * 4,
        scratch_shapes=[
            pltpu.VMEM((NX + 2, 32, 128), F32),
            pltpu.VMEM((NX, 32, 128), F32),
            pltpu.VMEM((NX, 32, 128), F32),
            pltpu.VMEM((own, NX, 256), F32),
            pltpu.VMEM((own, NX, 256), F32),
            pltpu.VMEM((own, NX, 256), F32),
            pltpu.VMEM(block, F32),
            pltpu.VMEM(block, F32),
            pltpu.VMEM((2, nk, NX, 256), F32),
            pltpu.VMEM((2, 8 * nk, 32, 128), F32),
            pltpu.VMEM((NX, 32, 128), F32),
            pltpu.VMEM((nk, 2, NX, 128), F32),
            pltpu.VMEM((tiles, 2) + block, F32),
            pltpu.VMEM((2, tiles) + block, F32),
            pltpu.VMEM((tiles,) + block, F32),
            pltpu.VMEM((2, tiles + 2) + block, F32),
            pltpu.VMEM((2,) + block, F32),
            pltpu.VMEM((2,) + block, F32),
            pltpu.VMEM((2, nj, 2 * own, NX, 128), F32),
            pltpu.VMEM((256, NX * 128), F32),
            pltpu.VMEM((8, 32, NX * 128), F32),
            pltpu.VMEM((8, NX * 128), F32),
            pltpu.VMEM((2, 40, 128), F32),
            pltpu.VMEM((2, 2, 40, 128), F32),
            pltpu.VMEM((2, 32, 128), F32),
            pltpu.VMEM((2, 2, 32, 128), F32),
            pltpu.VMEM((256, 256), BF),
            pltpu.VMEM((256, 256), BF),
            pltpu.VMEM((16, 256), BF),
            pltpu.VMEM((32, 128), F32),
            pltpu.VMEM((32, 128), F32),
            dma((6,)),
            dma((8,)),
            dma((2, nk, 2)),
            dma((7,)),
            dma((tiles,)),
            dma((tiles,)),
            dma((2, nj)),
            dma((nj,)),
            dma((2, 2)),
            dma((2,)),
            dma((2, 2)),
            dma((2,)),
            dma((2, tiles)),
            dma((tiles,)),
            dma((2, tiles + 2)),
            dma((tiles,)),
            dma((2,)),
            dma,
            dma((2, nj, 2 * own)),
            dma((nk, 2)),
        ],
        compiler_params=pltpu.CompilerParams(
            collective_id=0, has_side_effects=True, vmem_limit_bytes=56 * 2**20
        ),
    )(
        target,
        plane_xy,
        turn(plane_xz),
        plane_yz,
        first_xy,
        turn(first_xz),
        first_yz,
        second_xy,
        turn(second_xz),
        second_yz,
        w_hidden,
        jnp.concatenate(
            [b_hidden, w_output.astype(F32), b_output, jnp.zeros((63,), F32)]
        ).reshape(1, 128),
    )
    xy, mxy, vxy, gxy, yz, myz, vyz, gyz, xz, mxz, vxz, gxz = outs
    xy, mxy, vxy = adam(xy, mxy, vxy, gxy, *scales(1))
    yz, myz, vyz = adam(yz, myz, vyz, gyz, *scales(1))
    xz, mxz, vxz = (jnp.transpose(a, (2, 0, 1)) for a in adam(xz, mxz, vxz, gxz, *scales(1)))
    return (xy, xz, yz, mxy, mxz, myz, vxy, vxz, vyz)


def solution(mesh):
    piece = P(None, "gx", "gy")
    return jax.shard_map(
        functools.partial(per_device, mesh.shape["gx"] // 2, mesh.shape["gy"]),
        mesh=mesh,
        in_specs=(P("gx", None, "gy"),) + (piece,) * 9 + (P(),) * 4,
        out_specs=(piece,) * 9,
        check_vma=False,
    )
```

```python
import functools
import jax
import jax.numpy as jnp
from jax import lax
from jax.experimental import pallas as pl
from jax.experimental.pallas import tpu as pltpu
from jax.sharding import PartitionSpec as P

STEPS = 2
START = 20


BETA_ONE = 0.9
BETA_TWO = 0.99
LEARN_RATE = 0.01
EPSILON = 1e-08
NX = 16
F32 = jnp.float32
BF = jnp.bfloat16
MESH = pl.DeviceIdType.MESH


def grad_block(
    tt, side, low_chip, high_chip, low_row, high_row, s, tgt, xy, xz, yz, w1, w2, wo, bh, wv, b0, gxy, gxz, gyz, fbuf, dbuf, rbuf
):
    wide = NX * 128
    xt = jnp.transpose(
        jnp.concatenate([xz[s, low_chip][:, :128], xz[s, high_chip][:, 128:]], axis=1)
    )
    h1 = xt.astype(BF)
    r1 = xt - h1.astype(F32)
    h2 = r1.astype(BF)
    h3 = (r1 - h2.astype(F32)).astype(BF)
    parts = jnp.concatenate([h1, h2, h3], axis=1)
    place = lax.broadcasted_iota(jnp.int32, (3 * NX, 128), 0) % NX
    yzt = jnp.concatenate(
        [yz[s, pl.ds(low_row, 4)], yz[s, pl.ds(high_row, 4)]], axis=0
    ).reshape(256, 128)
    for x in range(NX):
        col = jnp.dot(parts, (place == x).astype(BF), preferred_element_type=F32)
        f = ((col * yzt).reshape(8, 32, 128) * xy[x + 1][None]).reshape(256, 128)
        fbuf[:, x * 128 : (x + 1) * 128] = f
    pre = jnp.dot(w1[...], fbuf[...].astype(BF), preferred_element_type=F32)
    q = pre.reshape(8, 32, wide) + jnp.concatenate([bh[...]] * NX, axis=-1)[None]
    t = 1.0 + jnp.tanh(q)
    h = q * t
    dbuf[...] = (t + h * (2.0 - t)) * jnp.concatenate([wv[...]] * NX, axis=-1)[None]
    out = jnp.dot(wo[...], h.reshape(256, wide).astype(BF), preferred_element_type=F32)[:8]
    low = lax.broadcasted_iota(jnp.int32, (8, 128), 0) < 4
    for x in range(NX):
        want = jnp.where(low, tgt[x, pl.ds(8 * low_chip, 8), :], tgt[x, pl.ds(8 * high_chip, 8), :])
        rbuf[:, x * 128 : (x + 1) * 128] = out[:, x * 128 : (x + 1) * 128] + b0 - want
    d = (dbuf[...] * rbuf[...][:, None, :]).reshape(256, wide)
    p = jnp.dot(w2[...], d.astype(BF), preferred_element_type=F32) * fbuf[...]
    acc = None
    for x in range(NX):
        px = p[:, x * 128 : (x + 1) * 128]
        acc = px if acc is None else acc + px
        gxy[x] += jnp.sum(px.reshape(8, 32, 128), axis=0)
        if x % 4 == 0:
            top = px.astype(BF)
            rest = (px - top.astype(F32)).astype(BF)
            row = sum(
                lax.dot_general(
                    jnp.ones((16, 128), BF), part, (((1,), (1,)), ((), ())), preferred_element_type=F32
                )[0:1]
                for part in (top, rest)
            )
        else:
            row = jnp.sum(px, axis=-1).reshape(1, 256)
        gxz[low_chip, 0, x : x + 1, :] = row[:, :128]
        gxz[high_chip, 1, x : x + 1, :] = row[:, 128:]
    halves = acc.reshape(2, 4, 32, 128)
    gyz[tt, 0, side] = halves[0]
    gyz[tt, 1, side] = halves[1]


def copy_to(src, dst, send, recv, device):
    return pltpu.make_async_remote_copy(
        src_ref=src,
        dst_ref=dst,
        send_sem=send,
        recv_sem=recv,
        device_id=device,
        device_id_type=MESH,
    )


def adam(plane, first, second, grads, scale_one, scale_two):
    first = BETA_ONE * first + (1.0 - BETA_ONE) * grads
    second = BETA_TWO * second + (1.0 - BETA_TWO) * grads * grads
    plane = plane - LEARN_RATE * (first * scale_one) / (jnp.sqrt(second * scale_two) + EPSILON)
    return (plane, first, second)


def scales(step):
    return (1.0 / (1.0 - BETA_ONE ** (START + 1 + step)), 1.0 / (1.0 - BETA_TWO ** (START + 1 + step)))


def fit_kernel(
    nk,
    nj,
    tgt, xy_in, xz_in, yz_in, mxy_in, mxz_in, myz_in, vxy_in, vxz_in, vyz_in, w_hidden, small,
    xy_out, mxy_out, vxy_out, gxy_out, yz_out, myz_out, vyz_out, gyz_out, xz_out, mxz_out, vxz_out, gxz_out,
    xyp, mxy, vxy, mxz, vxz, gradxz, myz, vyz, xza, yza, gxy, gxz, gyz, sib, total, chain, saved, ypart, xparts,
    fbuf, dbuf, rbuf, row_out, row_in, col_out, col_in, w1, w2, wo, bh, wv,
    load, store,
    yz_recv, yz_send, relay_send, pass_send, xz_recv, xz_send, row_recv, row_send, col_recv, col_send,
    sib_recv, sib_send, chain_recv, chain_send, ypart_recv, ypart_send, xpart_recv, xpart_send,
):
    i = lax.axis_index("gx")
    j = lax.axis_index("gy")
    nz = nk // 2
    tiles = 2 * nz
    k = i // 2
    core = i % 2
    other = 1 - core
    high = k // nz
    zc = k % nz
    toward = 1 - 2 * core
    own = nk // nj
    sibling = (2 * k + other, j)
    following = (2 * (high * nz + (zc + toward + nz) % nz) + core, j)
    preceding = (2 * (high * nz + (zc - toward + nz) % nz) + core, j)
    partner = (2 * ((1 - high) * nz + zc) + core, j)
    partner_other = (2 * ((1 - high) * nz + zc) + other, j)

    def near(plane, offset, c):
        return (2 * (plane * nz + (zc + offset + nz) % nz) + c, j)

    after_row = ((i + 1) % (2 * nk), j)
    before_row = ((i + 2 * nk - 1) % (2 * nk), j)
    border = (2 * ((k + toward * (-1) + nk) % nk) + other, j)
    b0 = small[:, 64:65]
    b_hidden = small[:, :32]
    w_output = small[:, 32:64]
    lane = lax.broadcasted_iota(jnp.int32, (32, 128), 1)

    def place(plane, zz, half):
        return 4 * ((zz * 2 + half) * 2 + plane)

    def row_of(device):
        chip = device // 2
        return place(chip // nz, chip % nz, device % 2)

    mine = row_of(i)

    def loop(low, top, body):
        def step(r, carry):
            body(r)
            return carry

        lax.fori_loop(low, top, step, 0)

    def load_rows(src, dst, first, count, n):
        loop(0, count, lambda r: pltpu.make_async_copy(src.at[:, r, :], dst.at[first + r], load.at[n]).start())

    def loaded(dst, first, count, n):
        whole = dst.at[pl.ds(first, count)]
        pltpu.make_async_copy(whole, whole, load.at[n]).wait()

    def store_rows(src, first, dst, count, n):
        loop(0, count, lambda r: pltpu.make_async_copy(src.at[first + r], dst.at[:, r, :], store.at[n]).start())

    def stored(src, first, count, n):
        whole = src.at[pl.ds(first, count)]
        pltpu.make_async_copy(whole, whole, store.at[n]).wait()

    loop(0, 4, lambda r: pltpu.make_async_copy(yz_in.at[:, r, :], yza.at[0, mine + r], load.at[1]).start())
    load_rows(xy_in, xyp, 1, NX, 0)
    load_rows(mxy_in, mxy, 0, NX, 2)
    load_rows(vxy_in, vxy, 0, NX, 3)
    load_rows(myz_in, myz, 0, 4, 4)
    load_rows(vyz_in, vyz, 0, 4, 5)

    barrier = pltpu.get_barrier_semaphore()

    def greet(device):
        pl.semaphore_signal(barrier, inc=1, device_id=device, device_id_type=MESH)

    targets = [sibling, partner, partner_other]
    for plane in (high, 1 - high):
        for c in (core, other):
            targets.append(near(plane, toward, c))
    for device in targets:
        greet(device)
    for device in (near(high, -toward, core), near(1 - high, -toward, core), border):
        greet(device)
    loop(1, nj, lambda r: greet((i, (j + r) % nj)))

    def gathered(src, n):
        return jnp.concatenate([src[:, 8 * n + z, :] for z in range(8)], axis=1)

    def spread(dst, n, values):
        for z in range(8):
            dst[:, 8 * n + z, :] = values[:, 32 * z : 32 * z + 32]

    for n in range(own):
        xza[0, j * own + n] = gathered(xz_in, n)
        mxz[n] = gathered(mxz_in, n)
        vxz[n] = gathered(vxz_in, n)

    def away(tt):
        return (tt + 1) % nz

    def my_z(tt):
        return (zc - toward * away(tt) + nz) % nz

    def other_z(tt):
        return (zc + toward * away(tt) + nz) % nz

    def yz_copy(s, device, slot):
        part = yza.at[s, pl.ds(mine, 4)]
        return copy_to(part, part, yz_send.at[slot], yz_recv.at[s, zc, core, 1 + high], device)

    def one_wait(s, zz, half, plane):
        part = yza.at[s, pl.ds(place(plane, zz, half), 4)]
        copy_to(
            part, part, yz_send.at[0], yz_recv.at[s, zz, half, 1 + plane], sibling
        ).wait_recv()

    def pair_of(s, zz, half):
        return yza.at[s, pl.ds(place(0, zz, half), 8)]

    def pair_wait(s, zz, half):
        part = pair_of(s, zz, half)
        copy_to(part, part, yz_send.at[0], yz_recv.at[s, zz, half, 0], sibling).wait_recv()

    def relay_copy(s, tt):
        part = pair_of(s, my_z(tt), core)
        return copy_to(part, part, relay_send.at[tt], yz_recv.at[s, my_z(tt), core, 0], sibling)

    def pass_copy(s, tt):
        part = pair_of(s, my_z(tt), core)
        return copy_to(part, part, pass_send.at[tt], yz_recv.at[s, my_z(tt), core, 0], following)

    def xz_copy(s, r):
        mine = xza.at[s, pl.ds(j * own, own)]
        return copy_to(mine, mine, xz_send.at[r], xz_recv.at[s, j], (i, (j + r) % nj))

    def xz_wait(s, r):
        peer = (j + r) % nj
        part = xza.at[s, pl.ds(peer * own, own)]
        copy_to(part, part, xz_send.at[0], xz_recv.at[s, peer], (i, peer)).wait_recv()

    def row_copy(s, side):
        return copy_to(
            row_out.at[side],
            row_in.at[s, side],
            row_send.at[side],
            row_recv.at[s, side],
            after_row if side == 0 else before_row,
        )

    def col_copy(s, side):
        device = (i, (j + 1) % nj) if side == 0 else (i, (j + nj - 1) % nj)
        return copy_to(
            col_out.at[side], col_in.at[s, side], col_send.at[side], col_recv.at[s, side], device
        )

    def sib_copy(s, tt):
        return copy_to(
            gyz.at[tt, other], sib.at[s, tt], sib_send.at[tt], sib_recv.at[s, tt], sibling
        )

    def last_copy(s, side):
        return copy_to(
            gyz.at[nz - 1, other, side],
            sib.at[s, nz - 1, side],
            sib_send.at[nz - 1 + side],
            sib_recv.at[s, nz - 1 + side],
            sibling,
        )

    def chain_copy(s, tt):
        return copy_to(
            total.at[tt], chain.at[s, tt + 1], chain_send.at[tt], chain_recv.at[s, tt + 1], following
        )

    def chain_wait(s, tt):
        part = chain.at[s, tt]
        copy_to(part, part, chain_send.at[0], chain_recv.at[s, tt], following).wait_recv()

    def ypart_copy(s):
        return copy_to(saved.at[1], ypart.at[s], ypart_send, ypart_recv.at[s], partner)

    def xpart_copy(s, r):
        peer = (j + r) % nj
        return copy_to(
            gxz.at[pl.ds(own * peer, own)],
            xparts.at[s, j],
            xpart_send.at[r],
            xpart_recv.at[s, j],
            (i, peer),
        )

    def xpart_wait(s, r):
        peer = (j + r) % nj
        slot = xparts.at[s, peer]
        copy_to(slot, slot, xpart_send.at[0], xpart_recv.at[s, peer], (i, peer)).wait_recv()

    def send_yz(s):
        for slot in (3, 4, 5, 6, 0, 1, 2):
            yz_copy(s, targets[slot], slot).start()

    def yz_sent():
        for slot in range(7):
            yz_copy(0, sibling, slot).wait_send()
        loop(0, nz - 2, lambda tt: pass_copy(0, tt).wait_send())
        loop(1, nz - 1, lambda tt: relay_copy(0, tt).wait_send())

    def send_xz(s):
        loop(1, nj, lambda r: xz_copy(s, r).start())

    def xz_sent():
        loop(1, nj, lambda r: xz_copy(0, r).wait_send())

    def send_borders(s):
        for side, x in ((0, NX - 1), (1, 0)):
            row_out[side, pl.ds(0, 32)] = xyp[x + 1]
            line = xza[s, pl.ds(j * own, own), x, :]
            row_out[side, pl.ds(32, own)] = line[:, :128]
            row_out[side, pl.ds(32 + own, own)] = line[:, 128:]
            row_copy(s, side).start()
        for side, last in ((0, 127), (1, 0)):
            cols = jnp.zeros((32, 128), F32)
            for n in range(NX + 4):
                piece = xyp[n + 1] if n < NX else yza[s, mine + n - NX]
                cols = jnp.where(lane == n, pltpu.roll(piece, (n - last + 128) % 128, 1), cols)
            col_out[side] = cols
            col_copy(s, side).start()

    def finish_pair(s, tt):
        sib_copy(s, tt).wait_recv()

        @pl.when(tt == 0)
        def _():
            total[tt] = gyz[tt, core] + sib[s, tt]

        @pl.when(tt > 0)
        def _():
            chain_wait(s, tt)
            total[tt] = gyz[tt, core] + sib[s, tt] + chain[s, tt]

        chain_copy(s, tt).start()

    def sent():
        for side in range(2):
            row_copy(0, side).wait_send()
            col_copy(0, side).wait_send()
        loop(0, nz - 1, lambda tt: sib_copy(0, tt).wait_send())
        loop(0, 2, lambda side: last_copy(0, side).wait_send())
        loop(0, nz - 1, lambda tt: chain_copy(0, tt).wait_send())
        ypart_copy(0).wait_send()
        loop(1, nj, lambda r: xpart_copy(0, r).wait_send())

    def one_step(s):
        gxy[...] = jnp.zeros_like(gxy)
        for plane in range(2):
            one_wait(s, my_z(0), core, plane)
        if nz > 2:
            pass_copy(s, 0).start()
        for plane in range(2):
            one_wait(s, other_z(0), other, plane)

        loop(1, nj, lambda r: xz_wait(s, r))

        def block(u):
            tt = u // 2
            side = u % 2
            t = away(tt)
            plane = (high + side + jnp.where(t == 0, 1, 0)) % 2
            low_z = (zc - t + nz) % nz
            high_z = (zc + t) % nz

            @pl.when((side == 0) & (tt > 0) & (tt < nz - 1))
            def _():
                pair_wait(s, other_z(tt), other)

            @pl.when(u == tiles - 2)
            def _():
                one_wait(s, zc, core, 1 - high)
                one_wait(s, zc, other, 1 - high)
                one_wait(s, zc, other, high)

            grad_block(
                tt, side, plane * nz + low_z, plane * nz + high_z,
                place(plane, low_z, 0), place(plane, high_z, 1),
                s, tgt, xyp, xza, yza, w1, w2, wo, bh, wv, b0, gxy, gxz, gyz, fbuf, dbuf, rbuf,
            )

            @pl.when(tt == nz - 1)
            def _():
                last_copy(s, side).start()

            @pl.when((side == 1) & (tt < nz - 1))
            def _():
                sib_copy(s, tt).start()

            @pl.when((side == 0) & (tt + 2 < nz))
            def _():
                pair_wait(s, my_z(tt + 1), core)
                relay_copy(s, tt + 1).start()

            @pl.when((side == 0) & (tt + 3 < nz))
            def _():
                pass_copy(s, tt + 1).start()

            @pl.when((side == 0) & (tt > 0))
            def _():
                finish_pair(s, tt - 1)

        loop(0, tiles, block)
        loop(1, nj, lambda r: xpart_copy(s, r).start())
        xparts[s, j] = gxz[pl.ds(own * j, own)]

        scale_one = jnp.where(s == 0, scales(0)[0], scales(1)[0])
        scale_two = jnp.where(s == 0, scales(0)[1], scales(1)[1])

        for side in range(2):
            row_copy(s, side).wait_recv()
            col_copy(s, side).wait_recv()
        chain_wait(s, nz - 1)
        last_copy(s, 0).wait_recv()
        saved[1] = gyz[nz - 1, core, 0] + sib[s, nz - 1, 0] + chain[s, nz - 1, 1]
        ypart_copy(s).start()

        before = col_in[s, 0]
        after = col_in[s, 1]

        def sides(plane, n):
            left = jnp.where(j == 0, plane, pltpu.roll(before, 128 - n, 1))
            left = jnp.where(lane == 0, left, pltpu.roll(plane, 1, 1))
            right = jnp.where(j == nj - 1, plane, pltpu.roll(after, 127 - n, 1))
            right = jnp.where(lane == 127, right, pltpu.roll(plane, 127, 1))
            return left + right

        xyp[0] = jnp.where(i == 0, xyp[1], row_in[s, 0, pl.ds(0, 32)])
        xyp[NX + 1] = jnp.where(i == 2 * nk - 1, xyp[NX], row_in[s, 1, pl.ds(0, 32)])

        def update_xy(x):
            plane = xyp[x + 1]
            rough = 4.0 * plane - xyp[x] - xyp[x + 2] - sides(plane, x)
            gxy[x] = gxy[x] / plane + rough

        loop(0, NX, update_xy)

        @pl.when(s == 1)
        def _():
            store_rows(gxy, 0, gxy_out, NX, 6)

        loop(1, nj, lambda r: xpart_wait(s, r))
        lane_xz = lax.broadcasted_iota(jnp.int32, (NX, 256), 1)
        spot_xz = lax.broadcasted_iota(jnp.int32, (NX, 256), 0)
        for n in range(own):
            zb = j * own + n
            plane = xza[s, zb]
            line = [
                jnp.concatenate(
                    [row_in[s, side, 32 + n : 33 + n], row_in[s, side, 32 + own + n : 33 + own + n]],
                    axis=1,
                )
                for side in range(2)
            ]
            up = jnp.where(i == 0, plane, jnp.broadcast_to(line[0], plane.shape))
            up = jnp.where(spot_xz == 0, up, pltpu.roll(plane, 1, 0))
            down = jnp.where(i == 2 * nk - 1, plane, jnp.broadcast_to(line[1], plane.shape))
            down = jnp.where(spot_xz == NX - 1, down, pltpu.roll(plane, NX - 1, 0))
            left = pltpu.roll(xza[s, jnp.maximum(zb - 1, 0)], 32, 1)
            left = jnp.where(zb == 0, plane, left)
            left = jnp.where(lane_xz < 32, left, pltpu.roll(plane, 32, 1))
            right = pltpu.roll(xza[s, jnp.minimum(zb + 1, nk - 1)], 224, 1)
            right = jnp.where(zb == nk - 1, plane, right)
            right = jnp.where(lane_xz >= 224, right, pltpu.roll(plane, 224, 1))
            terms = [
                jnp.concatenate([xparts[s, peer, n, 0], xparts[s, peer, n, 1]], axis=1)
                for peer in range(nj)
            ]
            grads = sum(terms) / plane + (4.0 * plane - up - down - left - right)
            gradxz[n] = grads

        @pl.when(s == 0)
        def _():
            for n in range(own):
                plane, mxz[n], vxz[n] = adam(
                    xza[0, j * own + n], mxz[n], vxz[n], gradxz[n], scale_one, scale_two
                )
                xza[1, j * own + n] = plane
            xz_sent()
            send_xz(1)

        def update_yz():
            last_copy(s, 1).wait_recv()
            copy_to(ypart.at[s], ypart.at[s], ypart_send, ypart_recv.at[s], partner).wait_recv()
            for n in range(4):
                plane = yza[s, mine + n]
                back = mine + n - 1 if n > 0 else jnp.where(i == 0, mine, row_of(jnp.maximum(i - 1, 0)) + 3)
                ahead = (
                    mine + n + 1
                    if n < 3
                    else jnp.where(i == 2 * nk - 1, mine + 3, row_of(jnp.minimum(i + 1, 2 * nk - 1)))
                )
                left = yza[s, back]
                right = yza[s, ahead]
                rough = 4.0 * plane - left - right - sides(plane, NX + n)
                term = gyz[nz - 1, core, 1, n] + sib[s, nz - 1, 1, n] + chain[s, nz - 1, 0, n] + ypart[s, n]
                saved[0, n] = term / plane + rough

        @pl.when(s == 0)
        def _():
            loaded(myz, 0, 4, 4)
            loaded(vyz, 0, 4, 5)
            update_yz()
            for n in range(4):
                yza[1, mine + n], myz[n], vyz[n] = adam(
                    yza[0, mine + n], myz[n], vyz[n], saved[0, n], scale_one, scale_two
                )
            yz_sent()
            send_yz(1)
            loaded(mxy, 0, NX, 2)
            loaded(vxy, 0, NX, 3)
            def step_xy(x):
                xyp[x + 1], mxy[x], vxy[x] = adam(
                    xyp[x + 1], mxy[x], vxy[x], gxy[x], scale_one, scale_two
                )

            loop(0, NX, step_xy)
            sent()
            send_borders(1)
            loop(
                0,
                4,
                lambda r: pltpu.make_async_copy(
                    yza.at[1, mine + r], yz_out.at[:, r, :], store.at[0]
                ).start(),
            )
            store_rows(myz, 0, myz_out, 4, 1)
            store_rows(vyz, 0, vyz_out, 4, 2)
            store_rows(xyp, 1, xy_out, NX, 3)
            store_rows(mxy, 0, mxy_out, NX, 4)
            store_rows(vxy, 0, vxy_out, NX, 5)

        @pl.when(s == 1)
        def _():
            for n in range(own):
                spread(xz_out, n, xza[1, j * own + n])
                spread(mxz_out, n, mxz[n])
                spread(vxz_out, n, vxz[n])
                spread(gxz_out, n, gradxz[n])
            update_yz()
            loop(
                0,
                4,
                lambda r: pltpu.make_async_copy(
                    saved.at[0, r], gyz_out.at[:, r, :], store.at[7]
                ).start(),
            )

    wide = w_hidden[...].astype(F32)
    turned = lax.dot_general(
        w_hidden[...],
        (lax.broadcasted_iota(jnp.int32, (32, 32), 0) == lax.broadcasted_iota(jnp.int32, (32, 32), 1)).astype(BF),
        (((0,), (0,)), ((), ())),
        preferred_element_type=F32,
    )
    same = (
        lax.broadcasted_iota(jnp.int32, (256, 256), 0) // 32
        == lax.broadcasted_iota(jnp.int32, (256, 256), 1) // 32
    )

    def blocks(a):
        a = jnp.concatenate([a] * 8, axis=1)
        return jnp.where(same, jnp.concatenate([a] * 8, axis=0), 0.0).astype(BF)

    w1[...] = blocks(0.5 * turned)
    w2[...] = blocks(wide)
    line_out = jnp.broadcast_to(jnp.concatenate([w_output] * 8, axis=1), (16, 256))
    wo[...] = jnp.where(
        lax.broadcasted_iota(jnp.int32, (16, 256), 0)
        == lax.broadcasted_iota(jnp.int32, (16, 256), 1) // 32,
        line_out,
        0.0,
    ).astype(BF)
    square = lax.broadcasted_iota(jnp.int32, (32, 32), 0) == lax.broadcasted_iota(jnp.int32, (32, 32), 1)

    def column(row):
        kept = jnp.where(square, jnp.broadcast_to(row, (32, 32)), 0.0)
        return jnp.broadcast_to(jnp.sum(kept, axis=1, keepdims=True), (32, 128))

    bh[...] = column(0.5 * b_hidden)
    wv[...] = column(0.5 * w_output)

    whole = yza.at[0, pl.ds(mine, 4)]
    pltpu.make_async_copy(whole, whole, load.at[1]).wait()
    pl.semaphore_wait(barrier, nj + 9)
    send_yz(0)
    send_xz(0)
    loaded(xyp, 1, NX, 0)
    send_borders(0)
    loop(0, STEPS, one_step)
    sent()
    xz_sent()
    yz_sent()
    whole_one = yza.at[1, pl.ds(mine, 4)]
    pltpu.make_async_copy(whole_one, whole_one, store.at[0]).wait()
    stored(myz, 0, 4, 1)
    stored(vyz, 0, 4, 2)
    stored(xyp, 1, NX, 3)
    stored(mxy, 0, NX, 4)
    stored(vxy, 0, NX, 5)
    stored(gxy, 0, NX, 6)
    pltpu.make_async_copy(saved.at[0], saved.at[0], store.at[7]).wait()


def per_device(
    nk,
    nj,
    target,
    plane_xy,
    plane_xz,
    plane_yz,
    first_xy,
    first_xz,
    first_yz,
    second_xy,
    second_xz,
    second_yz,
    w_hidden,
    b_hidden,
    w_output,
    b_output,
):
    own = nk // nj

    def turn(a):
        return jnp.transpose(a, (1, 2, 0))

    vm = pl.BlockSpec(memory_space=pltpu.VMEM)
    far = pl.BlockSpec(memory_space=pl.ANY)
    dma = pltpu.SemaphoreType.DMA
    nz = nk // 2
    block = (4, 32, 128)
    shapes = [(32, NX, 128)] * 4 + [(32, 4, 128)] * 4 + [(NX, 8 * own, 32)] * 4
    outs = pl.pallas_call(
        functools.partial(fit_kernel, nk, nj),
        out_shape=[jax.ShapeDtypeStruct(shape, F32) for shape in shapes],
        in_specs=[vm, far, vm, far, far, vm, far, far, vm, far, vm, vm],
        out_specs=[far] * 8 + [vm] * 4,
        scratch_shapes=[
            pltpu.VMEM((NX + 2, 32, 128), F32),
            pltpu.VMEM((NX, 32, 128), F32),
            pltpu.VMEM((NX, 32, 128), F32),
            pltpu.VMEM((own, NX, 256), F32),
            pltpu.VMEM((own, NX, 256), F32),
            pltpu.VMEM((own, NX, 256), F32),
            pltpu.VMEM(block, F32),
            pltpu.VMEM(block, F32),
            pltpu.VMEM((2, nk, NX, 256), F32),
            pltpu.VMEM((2, 8 * nk, 32, 128), F32),
            pltpu.VMEM((NX, 32, 128), F32),
            pltpu.VMEM((nk, 2, NX, 128), F32),
            pltpu.VMEM((nz, 2, 2) + block, F32),
            pltpu.VMEM((2, nz, 2) + block, F32),
            pltpu.VMEM((nz, 2) + block, F32),
            pltpu.VMEM((2, nz, 2) + block, F32),
            pltpu.VMEM((2,) + block, F32),
            pltpu.VMEM((2,) + block, F32),
            pltpu.VMEM((2, nj, own, 2, NX, 128), F32),
            pltpu.VMEM((256, NX * 128), F32),
            pltpu.VMEM((8, 32, NX * 128), F32),
            pltpu.VMEM((8, NX * 128), F32),
            pltpu.VMEM((2, 40, 128), F32),
            pltpu.VMEM((2, 2, 40, 128), F32),
            pltpu.VMEM((2, 32, 128), F32),
            pltpu.VMEM((2, 2, 32, 128), F32),
            pltpu.VMEM((256, 256), BF),
            pltpu.VMEM((256, 256), BF),
            pltpu.VMEM((16, 256), BF),
            pltpu.VMEM((32, 128), F32),
            pltpu.VMEM((32, 128), F32),
            dma((6,)),
            dma((8,)),
            dma((2, nz, 2, 3)),
            dma((7,)),
            dma((nz,)),
            dma((nz,)),
            dma((2, nj)),
            dma((nj,)),
            dma((2, 2)),
            dma((2,)),
            dma((2, 2)),
            dma((2,)),
            dma((2, nz + 1)),
            dma((nz + 1,)),
            dma((2, nz)),
            dma((nz,)),
            dma((2,)),
            dma,
            dma((2, nj)),
            dma((nj,)),
        ],
        compiler_params=pltpu.CompilerParams(
            collective_id=0, has_side_effects=True, vmem_limit_bytes=56 * 2**20
        ),
    )(
        target,
        plane_xy,
        turn(plane_xz),
        plane_yz,
        first_xy,
        turn(first_xz),
        first_yz,
        second_xy,
        turn(second_xz),
        second_yz,
        w_hidden,
        jnp.concatenate(
            [b_hidden, w_output.astype(F32), b_output, jnp.zeros((63,), F32)]
        ).reshape(1, 128),
    )
    xy, mxy, vxy, gxy, yz, myz, vyz, gyz, xz, mxz, vxz, gxz = outs
    xy, mxy, vxy = adam(xy, mxy, vxy, gxy, *scales(1))
    yz, myz, vyz = adam(yz, myz, vyz, gyz, *scales(1))
    xz, mxz, vxz = (jnp.transpose(a, (2, 0, 1)) for a in adam(xz, mxz, vxz, gxz, *scales(1)))
    return (xy, xz, yz, mxy, mxz, myz, vxy, vxz, vyz)


def solution(mesh):
    piece = P(None, "gx", "gy")
    return jax.shard_map(
        functools.partial(per_device, mesh.shape["gx"] // 2, mesh.shape["gy"]),
        mesh=mesh,
        in_specs=(P("gx", None, "gy"),) + (piece,) * 9 + (P(),) * 4,
        out_specs=(piece,) * 9,
        check_vma=False,
    )
```

```python
import functools
import jax
import jax.numpy as jnp
from jax import lax
from jax.experimental import pallas as pl
from jax.experimental.pallas import tpu as pltpu
from jax.sharding import PartitionSpec as P

STEPS = 2
START = 20


BETA_ONE = 0.9
BETA_TWO = 0.99
LEARN_RATE = 0.01
EPSILON = 1e-08
NX = 16
F32 = jnp.float32
BF = jnp.bfloat16
MESH = pl.DeviceIdType.MESH


def grad_block(
    tt, side, low_chip, high_chip, low_row, high_row, s, tgt, xy, xz, yz, w1, w2, wo, bh, wv, b0, gxy, gxz, gyz, fbuf, dbuf, rbuf
):
    wide = NX * 128
    xt = jnp.transpose(
        jnp.concatenate([xz[s, low_chip][:, :128], xz[s, high_chip][:, 128:]], axis=1)
    )
    h1 = xt.astype(BF)
    r1 = xt - h1.astype(F32)
    h2 = r1.astype(BF)
    h3 = (r1 - h2.astype(F32)).astype(BF)
    parts = jnp.concatenate([h1, h2, h3], axis=1)
    place = lax.broadcasted_iota(jnp.int32, (3 * NX, 128), 0) % NX
    yzt = jnp.concatenate(
        [yz[s, pl.ds(low_row, 4)], yz[s, pl.ds(high_row, 4)]], axis=0
    ).reshape(256, 128)
    for x in range(NX):
        col = jnp.dot(parts, (place == x).astype(BF), preferred_element_type=F32)
        f = ((col * yzt).reshape(8, 32, 128) * xy[x + 1][None]).reshape(256, 128)
        fbuf[:, x * 128 : (x + 1) * 128] = f
    pre = jnp.dot(w1[...], fbuf[...].astype(BF), preferred_element_type=F32)
    q = pre.reshape(8, 32, wide) + jnp.concatenate([bh[...]] * NX, axis=-1)[None]
    t = 1.0 + jnp.tanh(q)
    h = q * t
    dbuf[...] = (t + h * (2.0 - t)) * jnp.concatenate([wv[...]] * NX, axis=-1)[None]
    out = jnp.dot(wo[...], h.reshape(256, wide).astype(BF), preferred_element_type=F32)[:8]
    low = lax.broadcasted_iota(jnp.int32, (8, 128), 0) < 4
    for x in range(NX):
        want = jnp.where(low, tgt[x, pl.ds(8 * low_chip, 8), :], tgt[x, pl.ds(8 * high_chip, 8), :])
        rbuf[:, x * 128 : (x + 1) * 128] = out[:, x * 128 : (x + 1) * 128] + b0 - want
    d = (dbuf[...] * rbuf[...][:, None, :]).reshape(256, wide)
    p = jnp.dot(w2[...], d.astype(BF), preferred_element_type=F32) * fbuf[...]
    acc = None
    for x in range(NX):
        px = p[:, x * 128 : (x + 1) * 128]
        acc = px if acc is None else acc + px
        gxy[x] += jnp.sum(px.reshape(8, 32, 128), axis=0)
        if x % 4 == 0:
            top = px.astype(BF)
            rest = (px - top.astype(F32)).astype(BF)
            row = sum(
                lax.dot_general(
                    jnp.ones((16, 128), BF), part, (((1,), (1,)), ((), ())), preferred_element_type=F32
                )[0:1]
                for part in (top, rest)
            )
        else:
            row = jnp.sum(px, axis=-1).reshape(1, 256)
        gxz[low_chip, 0, x : x + 1, :] = row[:, :128]
        gxz[high_chip, 1, x : x + 1, :] = row[:, 128:]
    halves = acc.reshape(2, 4, 32, 128)
    gyz[tt, 0, side] = halves[0]
    gyz[tt, 1, side] = halves[1]


def copy_to(src, dst, send, recv, device):
    return pltpu.make_async_remote_copy(
        src_ref=src,
        dst_ref=dst,
        send_sem=send,
        recv_sem=recv,
        device_id=device,
        device_id_type=MESH,
    )


def adam(plane, first, second, grads, scale_one, scale_two):
    first = BETA_ONE * first + (1.0 - BETA_ONE) * grads
    second = BETA_TWO * second + (1.0 - BETA_TWO) * grads * grads
    plane = plane - LEARN_RATE * (first * scale_one) / (jnp.sqrt(second * scale_two) + EPSILON)
    return (plane, first, second)


def scales(step):
    return (1.0 / (1.0 - BETA_ONE ** (START + 1 + step)), 1.0 / (1.0 - BETA_TWO ** (START + 1 + step)))


def fit_kernel(
    nk,
    nj,
    tgt_in, xy_in, xz_in, yz_in, mxy_in, mxz_in, myz_in, vxy_in, vxz_in, vyz_in, w_hidden, small,
    xy_out, mxy_out, vxy_out, gxy_out, yz_out, myz_out, vyz_out, gyz_out, xz_out, mxz_out, vxz_out, gxz_out,
    xyp, mxy, vxy, mxz, vxz, gradxz, myz, vyz, xza, yza, gxy, gxz, gyz, sib, total, chain, saved, ypart, xparts,
    fbuf, dbuf, rbuf, row_out, row_in, col_out, col_in, w1, w2, wo, bh, wv,
    tgt, load, store,
    yz_recv, yz_send, relay_send, pass_send, xz_recv, xz_send, row_recv, row_send, col_recv, col_send,
    sib_recv, sib_send, chain_recv, chain_send, ypart_recv, ypart_send, xpart_recv, xpart_send,
):
    i = lax.axis_index("gx")
    j = lax.axis_index("gy")
    nz = nk // 2
    tiles = 2 * nz
    k = i // 2
    core = i % 2
    other = 1 - core
    high = k // nz
    zc = k % nz
    toward = 1 - 2 * core
    own = nk // nj
    sibling = (2 * k + other, j)
    following = (2 * (high * nz + (zc + toward + nz) % nz) + core, j)
    preceding = (2 * (high * nz + (zc - toward + nz) % nz) + core, j)
    partner = (2 * ((1 - high) * nz + zc) + core, j)
    partner_other = (2 * ((1 - high) * nz + zc) + other, j)

    def near(plane, offset, c):
        return (2 * (plane * nz + (zc + offset + nz) % nz) + c, j)

    after_row = ((i + 1) % (2 * nk), j)
    before_row = ((i + 2 * nk - 1) % (2 * nk), j)
    border = (2 * ((k + toward * (-1) + nk) % nk) + other, j)
    b0 = small[:, 64:65]
    b_hidden = small[:, :32]
    w_output = small[:, 32:64]
    lane = lax.broadcasted_iota(jnp.int32, (32, 128), 1)

    def place(plane, zz, half):
        return 4 * ((zz * 2 + half) * 2 + plane)

    def row_of(device):
        chip = device // 2
        return place(chip // nz, chip % nz, device % 2)

    mine = row_of(i)

    def loop(low, top, body):
        def step(r, carry):
            body(r)
            return carry

        lax.fori_loop(low, top, step, 0)

    def load_rows(src, dst, first, count, n):
        loop(0, count, lambda r: pltpu.make_async_copy(src.at[:, r, :], dst.at[first + r], load.at[n]).start())

    def loaded(dst, first, count, n):
        whole = dst.at[pl.ds(first, count)]
        pltpu.make_async_copy(whole, whole, load.at[n]).wait()

    def store_rows(src, first, dst, count, n):
        loop(0, count, lambda r: pltpu.make_async_copy(src.at[first + r], dst.at[:, r, :], store.at[n]).start())

    def stored(src, first, count, n):
        whole = src.at[pl.ds(first, count)]
        pltpu.make_async_copy(whole, whole, store.at[n]).wait()

    barrier = pltpu.get_barrier_semaphore()

    def greet(device):
        pl.semaphore_signal(barrier, inc=1, device_id=device, device_id_type=MESH)

    targets = [sibling, partner, partner_other]
    for plane in (high, 1 - high):
        for c in (core, other):
            targets.append(near(plane, toward, c))
    for device in targets:
        greet(device)
    for device in (near(high, -toward, core), near(1 - high, -toward, core), border):
        greet(device)
    loop(1, nj, lambda r: greet((i, (j + r) % nj)))
    loop(0, 4, lambda r: pltpu.make_async_copy(yz_in.at[:, r, :], yza.at[0, mine + r], load.at[1]).start())
    load_rows(xy_in, xyp, 1, NX, 0)
    pltpu.make_async_copy(tgt_in, tgt, load.at[6]).start()

    def gathered(src, n):
        return jnp.concatenate([src[:, 8 * n + z, :] for z in range(8)], axis=1)

    def spread(dst, n, values):
        for z in range(8):
            dst[:, 8 * n + z, :] = values[:, 32 * z : 32 * z + 32]

    for n in range(own):
        xza[0, j * own + n] = gathered(xz_in, n)
        mxz[n] = gathered(mxz_in, n)
        vxz[n] = gathered(vxz_in, n)

    def away(tt):
        return (tt + 1) % nz

    def my_z(tt):
        return (zc - toward * away(tt) + nz) % nz

    def other_z(tt):
        return (zc + toward * away(tt) + nz) % nz

    def yz_copy(s, device, slot):
        part = yza.at[s, pl.ds(mine, 4)]
        return copy_to(part, part, yz_send.at[slot], yz_recv.at[s, zc, core, 1 + high], device)

    def one_wait(s, zz, half, plane):
        part = yza.at[s, pl.ds(place(plane, zz, half), 4)]
        copy_to(
            part, part, yz_send.at[0], yz_recv.at[s, zz, half, 1 + plane], sibling
        ).wait_recv()

    def pair_of(s, zz, half):
        return yza.at[s, pl.ds(place(0, zz, half), 8)]

    def pair_wait(s, zz, half):
        part = pair_of(s, zz, half)
        copy_to(part, part, yz_send.at[0], yz_recv.at[s, zz, half, 0], sibling).wait_recv()

    def relay_copy(s, tt):
        part = pair_of(s, my_z(tt), core)
        return copy_to(part, part, relay_send.at[tt], yz_recv.at[s, my_z(tt), core, 0], sibling)

    def pass_copy(s, tt):
        part = pair_of(s, my_z(tt), core)
        return copy_to(part, part, pass_send.at[tt], yz_recv.at[s, my_z(tt), core, 0], following)

    def xz_copy(s, r):
        mine = xza.at[s, pl.ds(j * own, own)]
        return copy_to(mine, mine, xz_send.at[r], xz_recv.at[s, j], (i, (j + r) % nj))

    def xz_wait(s, r):
        peer = (j + r) % nj
        part = xza.at[s, pl.ds(peer * own, own)]
        copy_to(part, part, xz_send.at[0], xz_recv.at[s, peer], (i, peer)).wait_recv()

    def row_copy(s, side):
        return copy_to(
            row_out.at[side],
            row_in.at[s, side],
            row_send.at[side],
            row_recv.at[s, side],
            after_row if side == 0 else before_row,
        )

    def col_copy(s, side):
        device = (i, (j + 1) % nj) if side == 0 else (i, (j + nj - 1) % nj)
        return copy_to(
            col_out.at[side], col_in.at[s, side], col_send.at[side], col_recv.at[s, side], device
        )

    def sib_copy(s, tt):
        return copy_to(
            gyz.at[tt, other], sib.at[s, tt], sib_send.at[tt], sib_recv.at[s, tt], sibling
        )

    def last_copy(s, side):
        return copy_to(
            gyz.at[nz - 1, other, side],
            sib.at[s, nz - 1, side],
            sib_send.at[nz - 1 + side],
            sib_recv.at[s, nz - 1 + side],
            sibling,
        )

    def chain_copy(s, tt):
        return copy_to(
            total.at[tt], chain.at[s, tt + 1], chain_send.at[tt], chain_recv.at[s, tt + 1], following
        )

    def chain_wait(s, tt):
        part = chain.at[s, tt]
        copy_to(part, part, chain_send.at[0], chain_recv.at[s, tt], following).wait_recv()

    def ypart_copy(s):
        return copy_to(saved.at[1], ypart.at[s], ypart_send, ypart_recv.at[s], partner)

    def xpart_copy(s, r):
        peer = (j + r) % nj
        return copy_to(
            gxz.at[pl.ds(own * peer, own)],
            xparts.at[s, j],
            xpart_send.at[r],
            xpart_recv.at[s, j],
            (i, peer),
        )

    def xpart_wait(s, r):
        peer = (j + r) % nj
        slot = xparts.at[s, peer]
        copy_to(slot, slot, xpart_send.at[0], xpart_recv.at[s, peer], (i, peer)).wait_recv()

    def send_yz(s):
        for slot in (3, 4, 5, 6, 0, 1, 2):
            yz_copy(s, targets[slot], slot).start()

    def yz_sent():
        for slot in range(7):
            yz_copy(0, sibling, slot).wait_send()
        loop(0, nz - 2, lambda tt: pass_copy(0, tt).wait_send())
        loop(1, nz - 1, lambda tt: relay_copy(0, tt).wait_send())

    def send_xz(s):
        loop(1, nj, lambda r: xz_copy(s, r).start())

    def xz_sent():
        loop(1, nj, lambda r: xz_copy(0, r).wait_send())

    def send_borders(s):
        for side, x in ((0, NX - 1), (1, 0)):
            row_out[side, pl.ds(0, 32)] = xyp[x + 1]
            line = xza[s, pl.ds(j * own, own), x, :]
            row_out[side, pl.ds(32, own)] = line[:, :128]
            row_out[side, pl.ds(32 + own, own)] = line[:, 128:]
            row_copy(s, side).start()
        for side, last in ((0, 127), (1, 0)):
            cols = jnp.zeros((32, 128), F32)
            for n in range(NX + 4):
                piece = xyp[n + 1] if n < NX else yza[s, mine + n - NX]
                cols = jnp.where(lane == n, pltpu.roll(piece, (n - last + 128) % 128, 1), cols)
            col_out[side] = cols
            col_copy(s, side).start()

    def finish_pair(s, tt):
        sib_copy(s, tt).wait_recv()

        @pl.when(tt == 0)
        def _():
            total[tt] = gyz[tt, core] + sib[s, tt]

        @pl.when(tt > 0)
        def _():
            chain_wait(s, tt)
            total[tt] = gyz[tt, core] + sib[s, tt] + chain[s, tt]

        chain_copy(s, tt).start()

    def sent():
        for side in range(2):
            row_copy(0, side).wait_send()
            col_copy(0, side).wait_send()
        loop(0, nz - 1, lambda tt: sib_copy(0, tt).wait_send())
        loop(0, 2, lambda side: last_copy(0, side).wait_send())
        loop(0, nz - 1, lambda tt: chain_copy(0, tt).wait_send())
        ypart_copy(0).wait_send()
        loop(1, nj, lambda r: xpart_copy(0, r).wait_send())

    def one_step(s):
        gxy[...] = jnp.zeros_like(gxy)
        for plane in range(2):
            one_wait(s, my_z(0), core, plane)
        if nz > 2:
            pass_copy(s, 0).start()
        for plane in range(2):
            one_wait(s, other_z(0), other, plane)

        loop(1, nj, lambda r: xz_wait(s, r))

        def block(u):
            tt = u // 2
            side = u % 2
            t = away(tt)
            plane = (high + side + jnp.where(t == 0, 1, 0)) % 2
            low_z = (zc - t + nz) % nz
            high_z = (zc + t) % nz

            @pl.when((side == 0) & (tt > 0) & (tt < nz - 1))
            def _():
                pair_wait(s, other_z(tt), other)

            @pl.when(u == tiles - 2)
            def _():
                one_wait(s, zc, core, 1 - high)
                one_wait(s, zc, other, 1 - high)
                one_wait(s, zc, other, high)

            grad_block(
                tt, side, plane * nz + low_z, plane * nz + high_z,
                place(plane, low_z, 0), place(plane, high_z, 1),
                s, tgt, xyp, xza, yza, w1, w2, wo, bh, wv, b0, gxy, gxz, gyz, fbuf, dbuf, rbuf,
            )

            @pl.when(tt == nz - 1)
            def _():
                last_copy(s, side).start()

            @pl.when((side == 1) & (tt < nz - 1))
            def _():
                sib_copy(s, tt).start()

            @pl.when((side == 0) & (tt + 2 < nz))
            def _():
                pair_wait(s, my_z(tt + 1), core)
                relay_copy(s, tt + 1).start()

            @pl.when((side == 0) & (tt + 3 < nz))
            def _():
                pass_copy(s, tt + 1).start()

            @pl.when((side == 0) & (tt > 0))
            def _():
                finish_pair(s, tt - 1)

        loop(0, tiles, block)
        loop(1, nj, lambda r: xpart_copy(s, r).start())
        xparts[s, j] = gxz[pl.ds(own * j, own)]

        scale_one = jnp.where(s == 0, scales(0)[0], scales(1)[0])
        scale_two = jnp.where(s == 0, scales(0)[1], scales(1)[1])

        for side in range(2):
            row_copy(s, side).wait_recv()
            col_copy(s, side).wait_recv()
        chain_wait(s, nz - 1)
        last_copy(s, 0).wait_recv()
        saved[1] = gyz[nz - 1, core, 0] + sib[s, nz - 1, 0] + chain[s, nz - 1, 1]
        ypart_copy(s).start()

        before = col_in[s, 0]
        after = col_in[s, 1]

        def sides(plane, n):
            left = jnp.where(j == 0, plane, pltpu.roll(before, 128 - n, 1))
            left = jnp.where(lane == 0, left, pltpu.roll(plane, 1, 1))
            right = jnp.where(j == nj - 1, plane, pltpu.roll(after, 127 - n, 1))
            right = jnp.where(lane == 127, right, pltpu.roll(plane, 127, 1))
            return left + right

        xyp[0] = jnp.where(i == 0, xyp[1], row_in[s, 0, pl.ds(0, 32)])
        xyp[NX + 1] = jnp.where(i == 2 * nk - 1, xyp[NX], row_in[s, 1, pl.ds(0, 32)])

        def update_xy(x):
            plane = xyp[x + 1]
            rough = 4.0 * plane - xyp[x] - xyp[x + 2] - sides(plane, x)
            gxy[x] = gxy[x] / plane + rough

        loop(0, NX, update_xy)

        @pl.when(s == 1)
        def _():
            store_rows(gxy, 0, gxy_out, NX, 6)

        loop(1, nj, lambda r: xpart_wait(s, r))
        lane_xz = lax.broadcasted_iota(jnp.int32, (NX, 256), 1)
        spot_xz = lax.broadcasted_iota(jnp.int32, (NX, 256), 0)
        for n in range(own):
            zb = j * own + n
            plane = xza[s, zb]
            line = [
                jnp.concatenate(
                    [row_in[s, side, 32 + n : 33 + n], row_in[s, side, 32 + own + n : 33 + own + n]],
                    axis=1,
                )
                for side in range(2)
            ]
            up = jnp.where(i == 0, plane, jnp.broadcast_to(line[0], plane.shape))
            up = jnp.where(spot_xz == 0, up, pltpu.roll(plane, 1, 0))
            down = jnp.where(i == 2 * nk - 1, plane, jnp.broadcast_to(line[1], plane.shape))
            down = jnp.where(spot_xz == NX - 1, down, pltpu.roll(plane, NX - 1, 0))
            left = pltpu.roll(xza[s, jnp.maximum(zb - 1, 0)], 32, 1)
            left = jnp.where(zb == 0, plane, left)
            left = jnp.where(lane_xz < 32, left, pltpu.roll(plane, 32, 1))
            right = pltpu.roll(xza[s, jnp.minimum(zb + 1, nk - 1)], 224, 1)
            right = jnp.where(zb == nk - 1, plane, right)
            right = jnp.where(lane_xz >= 224, right, pltpu.roll(plane, 224, 1))
            terms = [
                jnp.concatenate([xparts[s, peer, n, 0], xparts[s, peer, n, 1]], axis=1)
                for peer in range(nj)
            ]
            grads = sum(terms) / plane + (4.0 * plane - up - down - left - right)
            gradxz[n] = grads

        @pl.when(s == 0)
        def _():
            for n in range(own):
                plane, mxz[n], vxz[n] = adam(
                    xza[0, j * own + n], mxz[n], vxz[n], gradxz[n], scale_one, scale_two
                )
                xza[1, j * own + n] = plane
            xz_sent()
            send_xz(1)

        def update_yz():
            last_copy(s, 1).wait_recv()
            copy_to(ypart.at[s], ypart.at[s], ypart_send, ypart_recv.at[s], partner).wait_recv()
            for n in range(4):
                plane = yza[s, mine + n]
                back = mine + n - 1 if n > 0 else jnp.where(i == 0, mine, row_of(jnp.maximum(i - 1, 0)) + 3)
                ahead = (
                    mine + n + 1
                    if n < 3
                    else jnp.where(i == 2 * nk - 1, mine + 3, row_of(jnp.minimum(i + 1, 2 * nk - 1)))
                )
                left = yza[s, back]
                right = yza[s, ahead]
                rough = 4.0 * plane - left - right - sides(plane, NX + n)
                term = gyz[nz - 1, core, 1, n] + sib[s, nz - 1, 1, n] + chain[s, nz - 1, 0, n] + ypart[s, n]
                saved[0, n] = term / plane + rough

        @pl.when(s == 0)
        def _():
            loaded(myz, 0, 4, 4)
            loaded(vyz, 0, 4, 5)
            update_yz()
            for n in range(4):
                yza[1, mine + n], myz[n], vyz[n] = adam(
                    yza[0, mine + n], myz[n], vyz[n], saved[0, n], scale_one, scale_two
                )
            yz_sent()
            send_yz(1)
            loaded(mxy, 0, NX, 2)
            loaded(vxy, 0, NX, 3)
            def step_xy(x):
                xyp[x + 1], mxy[x], vxy[x] = adam(
                    xyp[x + 1], mxy[x], vxy[x], gxy[x], scale_one, scale_two
                )

            loop(0, NX, step_xy)
            sent()
            send_borders(1)
            loop(
                0,
                4,
                lambda r: pltpu.make_async_copy(
                    yza.at[1, mine + r], yz_out.at[:, r, :], store.at[0]
                ).start(),
            )
            store_rows(myz, 0, myz_out, 4, 1)
            store_rows(vyz, 0, vyz_out, 4, 2)
            store_rows(xyp, 1, xy_out, NX, 3)
            store_rows(mxy, 0, mxy_out, NX, 4)
            store_rows(vxy, 0, vxy_out, NX, 5)

        @pl.when(s == 1)
        def _():
            for n in range(own):
                spread(xz_out, n, xza[1, j * own + n])
                spread(mxz_out, n, mxz[n])
                spread(vxz_out, n, vxz[n])
                spread(gxz_out, n, gradxz[n])
            update_yz()
            loop(
                0,
                4,
                lambda r: pltpu.make_async_copy(
                    saved.at[0, r], gyz_out.at[:, r, :], store.at[7]
                ).start(),
            )

    wide = w_hidden[...].astype(F32)
    turned = lax.dot_general(
        w_hidden[...],
        (lax.broadcasted_iota(jnp.int32, (32, 32), 0) == lax.broadcasted_iota(jnp.int32, (32, 32), 1)).astype(BF),
        (((0,), (0,)), ((), ())),
        preferred_element_type=F32,
    )
    same = (
        lax.broadcasted_iota(jnp.int32, (256, 256), 0) // 32
        == lax.broadcasted_iota(jnp.int32, (256, 256), 1) // 32
    )

    def blocks(a):
        a = jnp.concatenate([a] * 8, axis=1)
        return jnp.where(same, jnp.concatenate([a] * 8, axis=0), 0.0).astype(BF)

    w1[...] = blocks(0.5 * turned)
    w2[...] = blocks(wide)
    line_out = jnp.broadcast_to(jnp.concatenate([w_output] * 8, axis=1), (16, 256))
    wo[...] = jnp.where(
        lax.broadcasted_iota(jnp.int32, (16, 256), 0)
        == lax.broadcasted_iota(jnp.int32, (16, 256), 1) // 32,
        line_out,
        0.0,
    ).astype(BF)
    square = lax.broadcasted_iota(jnp.int32, (32, 32), 0) == lax.broadcasted_iota(jnp.int32, (32, 32), 1)

    def column(row):
        kept = jnp.where(square, jnp.broadcast_to(row, (32, 32)), 0.0)
        return jnp.broadcast_to(jnp.sum(kept, axis=1, keepdims=True), (32, 128))

    bh[...] = column(0.5 * b_hidden)
    wv[...] = column(0.5 * w_output)

    whole = yza.at[0, pl.ds(mine, 4)]
    pltpu.make_async_copy(whole, whole, load.at[1]).wait()
    pl.semaphore_wait(barrier, nj + 9)
    send_yz(0)
    send_xz(0)
    loaded(xyp, 1, NX, 0)
    send_borders(0)
    load_rows(mxy_in, mxy, 0, NX, 2)
    load_rows(vxy_in, vxy, 0, NX, 3)
    load_rows(myz_in, myz, 0, 4, 4)
    load_rows(vyz_in, vyz, 0, 4, 5)
    pltpu.make_async_copy(tgt_in, tgt, load.at[6]).wait()
    loop(0, STEPS, one_step)
    sent()
    xz_sent()
    yz_sent()
    whole_one = yza.at[1, pl.ds(mine, 4)]
    pltpu.make_async_copy(whole_one, whole_one, store.at[0]).wait()
    stored(myz, 0, 4, 1)
    stored(vyz, 0, 4, 2)
    stored(xyp, 1, NX, 3)
    stored(mxy, 0, NX, 4)
    stored(vxy, 0, NX, 5)
    stored(gxy, 0, NX, 6)
    pltpu.make_async_copy(saved.at[0], saved.at[0], store.at[7]).wait()


def per_device(
    nk,
    nj,
    target,
    plane_xy,
    plane_xz,
    plane_yz,
    first_xy,
    first_xz,
    first_yz,
    second_xy,
    second_xz,
    second_yz,
    w_hidden,
    b_hidden,
    w_output,
    b_output,
):
    own = nk // nj

    def turn(a):
        return jnp.transpose(a, (1, 2, 0))

    vm = pl.BlockSpec(memory_space=pltpu.VMEM)
    far = pl.BlockSpec(memory_space=pl.ANY)
    dma = pltpu.SemaphoreType.DMA
    nz = nk // 2
    block = (4, 32, 128)
    shapes = [(32, NX, 128)] * 4 + [(32, 4, 128)] * 4 + [(NX, 8 * own, 32)] * 4
    outs = pl.pallas_call(
        functools.partial(fit_kernel, nk, nj),
        out_shape=[jax.ShapeDtypeStruct(shape, F32) for shape in shapes],
        in_specs=[far, far, vm, far, far, vm, far, far, vm, far, vm, vm],
        out_specs=[far] * 8 + [vm] * 4,
        scratch_shapes=[
            pltpu.VMEM((NX + 2, 32, 128), F32),
            pltpu.VMEM((NX, 32, 128), F32),
            pltpu.VMEM((NX, 32, 128), F32),
            pltpu.VMEM((own, NX, 256), F32),
            pltpu.VMEM((own, NX, 256), F32),
            pltpu.VMEM((own, NX, 256), F32),
            pltpu.VMEM(block, F32),
            pltpu.VMEM(block, F32),
            pltpu.VMEM((2, nk, NX, 256), F32),
            pltpu.VMEM((2, 8 * nk, 32, 128), F32),
            pltpu.VMEM((NX, 32, 128), F32),
            pltpu.VMEM((nk, 2, NX, 128), F32),
            pltpu.VMEM((nz, 2, 2) + block, F32),
            pltpu.VMEM((2, nz, 2) + block, F32),
            pltpu.VMEM((nz, 2) + block, F32),
            pltpu.VMEM((2, nz, 2) + block, F32),
            pltpu.VMEM((2,) + block, F32),
            pltpu.VMEM((2,) + block, F32),
            pltpu.VMEM((2, nj, own, 2, NX, 128), F32),
            pltpu.VMEM((256, NX * 128), F32),
            pltpu.VMEM((8, 32, NX * 128), F32),
            pltpu.VMEM((8, NX * 128), F32),
            pltpu.VMEM((2, 40, 128), F32),
            pltpu.VMEM((2, 2, 40, 128), F32),
            pltpu.VMEM((2, 32, 128), F32),
            pltpu.VMEM((2, 2, 32, 128), F32),
            pltpu.VMEM((256, 256), BF),
            pltpu.VMEM((256, 256), BF),
            pltpu.VMEM((16, 256), BF),
            pltpu.VMEM((32, 128), F32),
            pltpu.VMEM((32, 128), F32),
            pltpu.VMEM((NX, 8 * nk, 128), F32),
            dma((7,)),
            dma((8,)),
            dma((2, nz, 2, 3)),
            dma((7,)),
            dma((nz,)),
            dma((nz,)),
            dma((2, nj)),
            dma((nj,)),
            dma((2, 2)),
            dma((2,)),
            dma((2, 2)),
            dma((2,)),
            dma((2, nz + 1)),
            dma((nz + 1,)),
            dma((2, nz)),
            dma((nz,)),
            dma((2,)),
            dma,
            dma((2, nj)),
            dma((nj,)),
        ],
        compiler_params=pltpu.CompilerParams(
            collective_id=0, has_side_effects=True, vmem_limit_bytes=56 * 2**20
        ),
    )(
        target,
        plane_xy,
        turn(plane_xz),
        plane_yz,
        first_xy,
        turn(first_xz),
        first_yz,
        second_xy,
        turn(second_xz),
        second_yz,
        w_hidden,
        jnp.concatenate(
            [b_hidden, w_output.astype(F32), b_output, jnp.zeros((63,), F32)]
        ).reshape(1, 128),
    )
    xy, mxy, vxy, gxy, yz, myz, vyz, gyz, xz, mxz, vxz, gxz = outs
    xy, mxy, vxy = adam(xy, mxy, vxy, gxy, *scales(1))
    yz, myz, vyz = adam(yz, myz, vyz, gyz, *scales(1))
    xz, mxz, vxz = (jnp.transpose(a, (2, 0, 1)) for a in adam(xz, mxz, vxz, gxz, *scales(1)))
    return (xy, xz, yz, mxy, mxz, myz, vxy, vxz, vyz)


def solution(mesh):
    piece = P(None, "gx", "gy")
    return jax.shard_map(
        functools.partial(per_device, mesh.shape["gx"] // 2, mesh.shape["gy"]),
        mesh=mesh,
        in_specs=(P("gx", None, "gy"),) + (piece,) * 9 + (P(),) * 4,
        out_specs=(piece,) * 9,
        check_vma=False,
    )
```
